128 devices in a mesh: space: 16 (over z, y), sub: 8 (over x, core).
Axes of the slice: x: 4, y: 4, z: 4, core: 2. Of those that a mesh axis runs over, the one named last changes fastest.
Arguments:
- coefficients: float32 [13, 20, 262144], P(None, None, ('space', 'sub')), may hold values from -6 to 6
- geometry: float32 [3, 3, 262144], P(None, None, ('space', 'sub')), may hold values from -3.5 to 3.5
- face_scale: float32 [4, 262144], P(None, ('space', 'sub')), may hold values from 0.3 to 1.5
- neighbours: int32 [4, 262144], P(None, ('space', 'sub')), may hold values from 0 to 2560, as said below
- stiffness: float32 [3, 20, 20], replicated, may hold values from -1.25 to 1.25
- face_minus: float32 [4, 20, 20], replicated, may hold values from -1.25 to 1.25
- face_plus: float32 [4, 20, 20], replicated, may hold values from -1.25 to 1.25
- jacobians: float32 [3, 13, 13], replicated, may hold values from -1.75 to 1.75
- flux_minus: float32 [13, 13], replicated, may hold values from -1.75 to 1.75
- flux_plus: float32 [13, 13], replicated, may hold values from -1.75 to 1.75
- face_basis: float32 [16, 20], replicated, may hold values from -1.25 to 1.25
- rotation: float32 [8, 13], replicated, may hold values from -1.75 to 1.75
- lift_quantity: float32 [13, 8], replicated, may hold values from -2 to 2
- lift_basis: float32 [20, 16], replicated, may hold values from -1.5 to 1.5
- send_elements: int32 [128, 128, 8], P(('space', 'sub')), may hold values from 0 to 2047, as said below
- send_count: int32 [128, 128], P(('space', 'sub')), may hold values from 0 to 8, as said below
- minus_slot: int32 [32768], P(('space', 'sub')), may hold values from 0 to 1023, as said below
- plus_slot: int32 [32768], P(('space', 'sub')), may hold values from 0 to 1023, as said below
- normal_stress: float32 [16, 32768], P(None, ('space', 'sub')), may hold values from -8 to -2
- shear_stress: float32 [2, 16, 32768], P(None, None, ('space', 'sub')), may hold values from 0.5 to 3
- pore_pressure: float32 [16, 32768], P(None, ('space', 'sub')), may hold values from 0.2 to 1.5
- initial_rate: float32 [16, 32768], P(None, ('space', 'sub')), may hold values from 0.05 to 2
- initial_state: float32 [16, 32768], P(None, ('space', 'sub')), may hold values from 0.45 to 0.7
- direct_effect: float32 [16, 32768], P(None, ('space', 'sub')), may hold values from 0.08 to 0.2
- evolution_effect: float32 [16, 32768], P(None, ('space', 'sub')), may hold values from 0.08 to 0.3
- slip_length: float32 [16, 32768], P(None, ('space', 'sub')), may hold values from 0.2 to 2
Outputs:
- updated: float32 [13, 20, 262144], P(None, None, ('space', 'sub'))
- slip_rate: float32 [16, 32768], P(None, ('space', 'sub'))
- fault_state: float32 [16, 32768], P(None, ('space', 'sub'))
The draws below stay inside these ranges and needn't reach their ends.
Inputs may be any that keep to these rules, and one draw needn't show every extreme that they name: `neighbours`: values index extended_p; the last face of every element named by a used slot (c < send_count) is the zero column 2560. `send_elements`: element indices within the sending partition; an element may stand in several slots. `send_count`: for every owner some partition fills all 8 slots of its block; the counts toward one owner sum to 512. For owner o, minus_slot and plus_slot of its 256 faces name 512 distinct slots s * 8 + c, exactly the used ones (c < send_count[s, o]). `plus_slot`: see minus_slot.
All inputs are finite; a program needn't handle non-finite values.
Results may differ from the reference program's by a relative error of at most 0.00045.
Values sent between devices are 32-bit elements; how exact they have to be, the bound alone decides.
No kernel may reach another device: no remote copies, remote signals or barrier semaphores. Data moves between devices by JAX's collectives and lax.ppermute only.
A program may use at most 128 MiB of HBM per device.

```python
import math
import jax
import jax.numpy as jnp
import numpy as np
from jax import lax

QUANT = 13
BASIS = 20
ORDER = 4
FACES = 4
POINTS = 16
TPOINTS = 4
FQUANT = 8
NEWTON = 6
ELEMS = 2048
GHOST = 256
FAULT_DEV = 256
PARTITIONS = 128
CAP = 8
ELEMS_ALL = 262144
FAULTS = 32768


def shuffle_row(row_key):
    return jax.random.permutation(row_key, 2 * FAULT_DEV).astype(jnp.int32)


def fault_layout(key):
    key = jax.random.fold_in(key, 101)
    level_key, stride_key, full_key, order_key, element_key = jax.random.split(key, 5)
    slot_total = PARTITIONS * CAP
    sources = jnp.arange(PARTITIONS, dtype=jnp.int32)
    level_root = jax.random.randint(level_key, (PARTITIONS, PARTITIONS), 0, 16)
    source_level = level_root * level_root
    chosen_full = jax.random.randint(full_key, (PARTITIONS,), 0, PARTITIONS)
    source_level = jnp.where(sources[None, :] == chosen_full[:, None], 300, source_level)
    stride = jax.random.randint(stride_key, (PARTITIONS, 1, 1), 1, 8)
    slot_score = source_level[:, :, None] * 16 - jnp.arange(CAP, dtype=jnp.int32)[None, None, :] * stride
    ranked = slot_score * slot_total + jnp.arange(slot_total, dtype=jnp.int32).reshape(1, PARTITIONS, CAP)
    unused_values, chosen = lax.top_k(ranked.reshape(PARTITIONS, slot_total), 2 * FAULT_DEV)
    chosen = chosen.astype(jnp.int32)
    counts = jnp.sum(((chosen // CAP)[:, :, None] == sources[None, None, :]).astype(jnp.int32), axis=1)
    orders = jax.vmap(shuffle_row)(jax.random.split(order_key, PARTITIONS))
    arranged = jnp.take_along_axis(chosen, orders, axis=1)
    minus_slot = arranged[:, :FAULT_DEV].reshape(-1)
    plus_slot = arranged[:, FAULT_DEV:].reshape(-1)
    send_elements = jax.random.randint(element_key, (PARTITIONS, PARTITIONS, CAP), 0, ELEMS)
    return (send_elements, jnp.transpose(counts), minus_slot, plus_slot)


def draw_send_elements(key, part):
    return fault_layout(key)[0]


def draw_send_count(key, part):
    return fault_layout(key)[1]


def draw_minus_slot(key, part):
    return fault_layout(key)[2]


def draw_plus_slot(key, part):
    return fault_layout(key)[3]


def draw_neighbours(key, part):
    send_elements, send_count, unused_minus, unused_plus = fault_layout(key)
    key = jax.random.fold_in(key, 7)
    table = jax.random.randint(key, (FACES, ELEMS_ALL), 0, ELEMS + 2 * GHOST)
    used = jnp.arange(CAP, dtype=jnp.int32)[None, None, :] < send_count[:, :, None]
    target = send_elements + jnp.arange(PARTITIONS, dtype=jnp.int32)[:, None, None] * ELEMS
    target = jnp.where(used, target, ELEMS_ALL)
    return table.at[FACES - 1, target.reshape(-1)].set(ELEMS + 2 * GHOST, mode='drop')


def steps_of(own_key, extent, cuts, smallest, largest):
    level, own = 1.0, jax.random.fold_in(own_key, 6)
    for axis_at, blocks in cuts:
        heights = jnp.exp(jax.random.uniform(jax.random.fold_in(own, axis_at), (blocks,), jnp.float32, smallest / len(cuts), largest / len(cuts)))
        level = level * jnp.repeat(heights, extent[axis_at] // blocks).reshape([-1 if axis == axis_at else 1 for axis in range(len(extent))])
    return level


def centred(own_key, extent, deviation, most, cuts=(), kind=jnp.bfloat16):
    values = deviation * jax.random.normal(own_key, extent, jnp.float32)
    if cuts:
        values = values * steps_of(own_key, extent, cuts, -0.22, 0.18)
    return jnp.clip(values, -most, most).astype(kind)


def setup_inputs(seed: int = 0) -> dict:
    splits = jax.random.split(jax.random.key(seed), 27)
    return {
        "coefficients": centred(splits[0], (QUANT, BASIS, ELEMS_ALL), 1.0, 6.0, ((2, 128),), jnp.float32),
        "geometry": centred(splits[1], (3, 3, ELEMS_ALL), 3 ** -0.5, 3.5, ((2, 128),), jnp.float32),
        "face_scale": jnp.clip(jnp.exp(math.log(1.5) - 1.60943787 * jax.random.uniform(splits[2], (FACES, ELEMS_ALL), jnp.float32) ** steps_of(splits[2], (FACES, ELEMS_ALL), ((1, 128),), -0.2, 0.2)), 0.3, 1.5),
        "neighbours": draw_neighbours(jax.random.fold_in(splits[26], 71), 0),
        "stiffness": centred(splits[4], (3, BASIS, BASIS), BASIS ** -0.5, 1.25, (), jnp.float32),
        "face_minus": centred(splits[5], (FACES, BASIS, BASIS), BASIS ** -0.5, 1.25, (), jnp.float32),
        "face_plus": centred(splits[6], (FACES, BASIS, BASIS), BASIS ** -0.5, 1.25, (), jnp.float32),
        "jacobians": centred(splits[7], (3, QUANT, QUANT), QUANT ** -0.5, 1.75, (), jnp.float32),
        "flux_minus": centred(splits[8], (QUANT, QUANT), QUANT ** -0.5, 1.75, (), jnp.float32),
        "flux_plus": centred(splits[9], (QUANT, QUANT), QUANT ** -0.5, 1.75, (), jnp.float32),
        "face_basis": centred(splits[10], (POINTS, BASIS), BASIS ** -0.5, 1.25, (), jnp.float32),
        "rotation": centred(splits[11], (FQUANT, QUANT), QUANT ** -0.5, 1.75, (), jnp.float32),
        "lift_quantity": centred(splits[12], (QUANT, FQUANT), FQUANT ** -0.5, 2.0, (), jnp.float32),
        "lift_basis": centred(splits[13], (BASIS, POINTS), POINTS ** -0.5, 1.5, (), jnp.float32),
        "send_elements": draw_send_elements(jax.random.fold_in(splits[26], 71), 0),
        "send_count": draw_send_count(jax.random.fold_in(splits[26], 71), 0),
        "minus_slot": draw_minus_slot(jax.random.fold_in(splits[26], 71), 0),
        "plus_slot": draw_plus_slot(jax.random.fold_in(splits[26], 71), 0),
        "normal_stress": jnp.clip(-8.0 + 6.0 * jax.random.uniform(splits[18], (POINTS, FAULTS), jnp.float32) ** steps_of(splits[18], (POINTS, FAULTS), ((1, 128),), -0.2, 0.2), -8.0, -2.0),
        "shear_stress": jnp.clip(0.5 + 2.5 * jax.random.uniform(splits[19], (2, POINTS, FAULTS), jnp.float32) ** steps_of(splits[19], (2, POINTS, FAULTS), ((2, 128),), -0.2, 0.2), 0.5, 3.0),
        "pore_pressure": jnp.clip(0.2 + 1.3 * jax.random.uniform(splits[20], (POINTS, FAULTS), jnp.float32) ** steps_of(splits[20], (POINTS, FAULTS), ((1, 128),), -0.2, 0.2), 0.2, 1.5),
        "initial_rate": jnp.clip(jnp.exp(math.log(2.0) - 3.6888794 * jax.random.uniform(splits[21], (POINTS, FAULTS), jnp.float32) ** steps_of(splits[21], (POINTS, FAULTS), ((1, 128),), -0.2, 0.2)), 0.05, 2.0),
        "initial_state": jnp.clip(0.45 + 0.25 * jax.random.uniform(splits[22], (POINTS, FAULTS), jnp.float32) ** steps_of(splits[22], (POINTS, FAULTS), ((1, 128),), -0.2, 0.2), 0.45, 0.7),
        "direct_effect": jnp.clip(jnp.exp(math.log(0.2) - 0.91629077 * jax.random.uniform(splits[23], (POINTS, FAULTS), jnp.float32) ** steps_of(splits[23], (POINTS, FAULTS), ((1, 128),), -0.2, 0.2)), 0.08, 0.2),
        "evolution_effect": jnp.clip(jnp.exp(math.log(0.3) - 1.3217559 * jax.random.uniform(splits[24], (POINTS, FAULTS), jnp.float32) ** steps_of(splits[24], (POINTS, FAULTS), ((1, 128),), -0.2, 0.2)), 0.08, 0.3),
        "slip_length": jnp.clip(jnp.exp(math.log(2.0) - 2.3025851 * jax.random.uniform(splits[25], (POINTS, FAULTS), jnp.float32) ** steps_of(splits[25], (POINTS, FAULTS), ((1, 128),), -0.2, 0.2)), 0.2, 2.0),
    }


highest = lax.Precision.HIGHEST
time_step = 0.5
friction_ref = 0.6
impedance_normal = 2.0
impedance_shear = 1.2
impedance_fluid = 0.8
rate_floor = 0.01
gauss_inner = 0.3399810435848563
gauss_outer = 0.8611363115940526
weight_inner = 0.6521451548625461
weight_outer = 0.3478548451374538

def time_tables(number):
    gauss_nodes = [-gauss_outer, -gauss_inner, gauss_inner, gauss_outer]
    gauss_weights = [weight_outer, weight_inner, weight_inner, weight_outer]
    time_points = [time_step * (1.0 + node_value) / 2.0 for node_value in gauss_nodes]
    widths = [time_step * weight_value / 2.0 for weight_value in gauss_weights]
    taylor = np.array([[point_value ** power / math.factorial(power) for power in range(ORDER)] for point_value in time_points])
    return (jnp.asarray(taylor, jnp.float32), [float(width_value) for width_value in widths])

def inverse_sinh(value):
    magnitude = jnp.abs(value)
    result = jnp.log(magnitude + jnp.sqrt(magnitude * magnitude + 1.0))
    return jnp.where(value < 0.0, -result, result)

def directional(field, geometry, jacobians):
    mixed_terms = jnp.einsum('xpq,qbe->xpbe', jacobians, field, precision=highest)
    return jnp.stack([geometry[axis_dir, 0] * mixed_terms[0] + geometry[axis_dir, 1] * mixed_terms[1] + geometry[axis_dir, 2] * mixed_terms[2] for axis_dir in range(3)])

def predictor(own_block, geometry, stiffness, jacobians):
    derivs = [own_block]
    for power in range(ORDER - 1):
        directed = directional(derivs[-1], geometry, jacobians)
        derivs.append(-jnp.einsum('dbc,dqce->qbe', stiffness, directed, precision=highest))
    integrated = jnp.zeros_like(own_block)
    for power in range(ORDER):
        integrated = integrated + time_step ** (power + 1) / math.factorial(power + 1) * derivs[power]
    return (derivs, integrated)

def volume_term(integrated, geometry, stiffness, jacobians):
    directed = directional(integrated, geometry, jacobians)
    return jnp.einsum('dcb,dqce->qbe', stiffness, directed, precision=highest)

def face_terms(integrated, extended, own_neighbours, own_scale, face_minus, face_plus, flux_minus, flux_plus):
    own_state = jnp.einsum('pq,qce->pce', flux_minus, integrated, precision=highest)
    far_state = jnp.einsum('pq,qce->pce', flux_plus, extended, precision=highest)
    flux_total = jnp.zeros_like(integrated)
    for face_index in range(FACES):
        beside = jnp.take(far_state, own_neighbours[face_index], axis=2)
        local_part = jnp.einsum('bc,pce->pbe', face_minus[face_index], own_state, precision=highest)
        far_part = jnp.einsum('bc,pce->pbe', face_plus[face_index], beside, precision=highest)
        flux_total = flux_total + own_scale[face_index] * (local_part + far_part)
    return flux_total

def fault_traces(derivs, slot_elements, face_basis, rotation, taylor):
    picked = jnp.stack([jnp.take(derivative, slot_elements, axis=2) for derivative in derivs])
    on_face = jnp.einsum('pb,kqbs->kqps', face_basis, picked, precision=highest)
    rotated = jnp.einsum('jq,kqps->kjps', rotation, on_face, precision=highest)
    return jnp.einsum('tk,kjps->sjtp', taylor, rotated, precision=highest)

def friction(trace_minus, trace_plus, normal_stress, shear_stress, pore_pressure, initial_rate, initial_state, direct_effect, evolution_effect, slip_length, widths):
    damping = 0.5 * impedance_shear
    slip_rate = initial_rate
    state_now = initial_state
    back_minus = jnp.zeros(trace_minus[:, 0].shape, jnp.float32)
    back_plus = jnp.zeros(trace_plus[:, 0].shape, jnp.float32)
    for point_index in range(TPOINTS):
        minus_now = trace_minus[:, point_index]
        plus_now = trace_plus[:, point_index]
        normal_mid = 0.5 * (minus_now[0] + plus_now[0]) + 0.5 * impedance_normal * (plus_now[3] - minus_now[3])
        shear_one = 0.5 * (minus_now[1] + plus_now[1]) + 0.5 * impedance_shear * (plus_now[4] - minus_now[4])
        shear_two = 0.5 * (minus_now[2] + plus_now[2]) + 0.5 * impedance_shear * (plus_now[5] - minus_now[5])
        fluid_mid = 0.5 * (minus_now[6] + plus_now[6]) + 0.5 * impedance_fluid * (plus_now[7] - minus_now[7])
        effective = jnp.maximum(-(normal_stress + normal_mid + pore_pressure + fluid_mid), 0.0)
        total_one = shear_stress[0] + shear_one
        total_two = shear_stress[1] + shear_two
        locked = jnp.sqrt(total_one * total_one + total_two * total_two + 1.0)
        scaled = 0.5 * jnp.exp(state_now / direct_effect)
        floor_term = 4.0 * jnp.exp(-2.0 * state_now / direct_effect)
        for sweep in range(NEWTON):
            residual = effective * direct_effect * inverse_sinh(scaled * slip_rate) + damping * slip_rate - locked
            slope_value = effective * direct_effect / jnp.sqrt(floor_term + slip_rate * slip_rate) + damping
            slip_rate = slip_rate - residual / slope_value
        steady = friction_ref - (evolution_effect - direct_effect) * 0.5 * jnp.log(slip_rate * slip_rate + rate_floor)
        state_now = steady + (state_now - steady) * jnp.exp(-jnp.abs(slip_rate) * widths[point_index] / slip_length)
        strength = locked - damping * slip_rate
        traction_one = strength * total_one / locked - shear_stress[0]
        traction_two = strength * total_two / locked - shear_stress[1]
        imposed_minus = jnp.stack([normal_mid, traction_one, traction_two, minus_now[3] + (normal_mid - minus_now[0]) / impedance_normal, minus_now[4] + (traction_one - minus_now[1]) / impedance_shear, minus_now[5] + (traction_two - minus_now[2]) / impedance_shear, fluid_mid, minus_now[7] + (fluid_mid - minus_now[6]) / impedance_fluid])
        imposed_plus = jnp.stack([normal_mid, traction_one, traction_two, plus_now[3] - (normal_mid - plus_now[0]) / impedance_normal, plus_now[4] - (traction_one - plus_now[1]) / impedance_shear, plus_now[5] - (traction_two - plus_now[2]) / impedance_shear, fluid_mid, plus_now[7] - (fluid_mid - plus_now[6]) / impedance_fluid])
        back_minus = back_minus + widths[point_index] * (imposed_minus - minus_now)
        back_plus = back_plus + widths[point_index] * (imposed_plus - plus_now)
    return (slip_rate, state_now, back_minus, back_plus)

def add_lift(updated, back, slot_elements, own_scale, lift_quantity, lift_basis):
    values = back.reshape(-1, FQUANT, POINTS)
    lifted = jnp.einsum('qi,bk,sik->qbs', lift_quantity, lift_basis, values, precision=highest)
    lifted = lifted * jnp.take(own_scale[FACES - 1], slot_elements)
    return updated.at[:, :, slot_elements].add(lifted)

def reference(coefficients, geometry, face_scale, neighbours, stiffness, face_minus, face_plus, jacobians, flux_minus, flux_plus, face_basis, rotation, lift_quantity, lift_basis, send_elements, send_count, minus_slot, plus_slot, normal_stress, shear_stress, pore_pressure, initial_rate, initial_state, direct_effect, evolution_effect, slip_length):
    part_count = send_count.shape[0]
    capacity = send_elements.shape[2]
    taylor, widths = time_tables(TPOINTS)
    trace_width = FQUANT * TPOINTS * POINTS
    coeff_blocks = coefficients.reshape(QUANT, BASIS, part_count, ELEMS)
    geometry_blocks = geometry.reshape(3, 3, part_count, ELEMS)
    scale_blocks = face_scale.reshape(FACES, part_count, ELEMS)
    neighbour_blocks = neighbours.reshape(FACES, part_count, ELEMS)

    def first_pass(part_index):
        own_block = lax.dynamic_index_in_dim(coeff_blocks, part_index, 2, keepdims=False)
        own_geometry = lax.dynamic_index_in_dim(geometry_blocks, part_index, 2, keepdims=False)
        derivs, integrated = predictor(own_block, own_geometry, stiffness, jacobians)
        slot_elements = lax.dynamic_index_in_dim(send_elements, part_index, 0, keepdims=False).reshape(-1)
        counts_here = lax.dynamic_index_in_dim(send_count, part_index, 0, keepdims=False)
        traces = fault_traces(derivs, slot_elements, face_basis, rotation, taylor).reshape(part_count, capacity, trace_width)
        filled = (jnp.arange(capacity, dtype=jnp.int32)[None, :] < counts_here[:, None]).astype(jnp.float32)
        return (integrated, traces * filled[:, :, None])
    integrated_all, traces_all = lax.map(first_pass, jnp.arange(part_count, dtype=jnp.int32))
    received_all = jnp.transpose(traces_all, (1, 0, 2, 3)).reshape(part_count, part_count * capacity, trace_width)
    owner_of = jnp.arange(minus_slot.shape[0], dtype=jnp.int32) // FAULT_DEV
    minus_rows = received_all[owner_of, minus_slot]
    plus_rows = received_all[owner_of, plus_slot]
    trace_minus = jnp.transpose(minus_rows.reshape(-1, FQUANT, TPOINTS, POINTS), (1, 2, 3, 0))
    trace_plus = jnp.transpose(plus_rows.reshape(-1, FQUANT, TPOINTS, POINTS), (1, 2, 3, 0))
    slip_rate, fault_state, back_minus, back_plus = friction(trace_minus, trace_plus, normal_stress, shear_stress, pore_pressure, initial_rate, initial_state, direct_effect, evolution_effect, slip_length, widths)
    rows_minus = jnp.transpose(back_minus, (2, 0, 1)).reshape(-1, FQUANT * POINTS)
    rows_plus = jnp.transpose(back_plus, (2, 0, 1)).reshape(-1, FQUANT * POINTS)
    returned = jnp.zeros((part_count, part_count * capacity, FQUANT * POINTS), jnp.float32)
    returned = returned.at[owner_of, minus_slot].set(rows_minus).at[owner_of, plus_slot].set(rows_plus)
    returned = returned.reshape(part_count, part_count, capacity, FQUANT * POINTS)

    def second_pass(part_index):
        own_block = lax.dynamic_index_in_dim(coeff_blocks, part_index, 2, keepdims=False)
        own_geometry = lax.dynamic_index_in_dim(geometry_blocks, part_index, 2, keepdims=False)
        own_scale = lax.dynamic_index_in_dim(scale_blocks, part_index, 1, keepdims=False)
        own_neighbours = lax.dynamic_index_in_dim(neighbour_blocks, part_index, 1, keepdims=False)
        integrated = lax.dynamic_index_in_dim(integrated_all, part_index, 0, keepdims=False)
        lower_rim = lax.dynamic_index_in_dim(integrated_all, jnp.maximum(part_index - 1, 0), 0, keepdims=False)[:, :, ELEMS - GHOST:]
        upper_rim = lax.dynamic_index_in_dim(integrated_all, jnp.minimum(part_index + 1, part_count - 1), 0, keepdims=False)[:, :, :GHOST]
        lower_rim = jnp.where(part_index > 0, lower_rim, 0.0)
        upper_rim = jnp.where(part_index < part_count - 1, upper_rim, 0.0)
        extended = jnp.concatenate([lower_rim, integrated, upper_rim, jnp.zeros((QUANT, BASIS, 1), jnp.float32)], axis=2)
        updated = own_block + volume_term(integrated, own_geometry, stiffness, jacobians) - face_terms(integrated, extended, own_neighbours, own_scale, face_minus, face_plus, flux_minus, flux_plus)
        back = lax.dynamic_index_in_dim(returned, part_index, 1, keepdims=False)
        slot_elements = lax.dynamic_index_in_dim(send_elements, part_index, 0, keepdims=False).reshape(-1)
        return add_lift(updated, back, slot_elements, own_scale, lift_quantity, lift_basis)
    blocks = lax.map(second_pass, jnp.arange(part_count, dtype=jnp.int32))
    updated = jnp.transpose(blocks, (1, 2, 0, 3)).reshape(QUANT, BASIS, part_count * ELEMS)
    return (updated, slip_rate, fault_state)
```

```python
import math

import jax
import jax.numpy as jnp
import numpy as np
from jax import lax
from jax.experimental import pallas as pl
from jax.experimental.pallas import tpu as pltpu
from jax.sharding import PartitionSpec as P

QUANT = 13
BASIS = 20
ORDER = 4
FACES = 4
POINTS = 16
TPOINTS = 4
FQUANT = 8
NEWTON = 6
GHOST = 256
COLS = 512
MAIN_COLS = 1024

time_step = 0.5
friction_ref = 0.6
impedance_normal = 2.0
impedance_shear = 1.2
impedance_fluid = 0.8
rate_floor = 0.01
gauss_inner = 0.3399810435848563
gauss_outer = 0.8611363115940526
weight_inner = 0.6521451548625461
weight_outer = 0.3478548451374538

f32 = jnp.float32
bf16 = jnp.bfloat16
AXES = ("space", "sub")
VMEM_LIMIT = 56 * 1024 * 1024

QUADS = 5
PAIRS = 7
ROWS = 280
QUAD_ROWS = 56
PAIR_ROWS = 40


def pair_tiles(p):
    return [PAIRS * k + p for k in range(QUADS)]


GROUPS = tuple([t for p in pairs for t in pair_tiles(p)] for pairs in ((0, 1), (2, 3), (4, 5, 6)))


def time_tables():
    gauss_nodes = [-gauss_outer, -gauss_inner, gauss_inner, gauss_outer]
    gauss_weights = [weight_outer, weight_inner, weight_inner, weight_outer]
    time_points = [time_step * (1.0 + node_value) / 2.0 for node_value in gauss_nodes]
    widths = [time_step * weight_value / 2.0 for weight_value in gauss_weights]
    taylor = [
        [float(np.float32(point_value**power / math.factorial(power))) for power in range(ORDER)]
        for point_value in time_points
    ]
    return taylor, [float(width_value) for width_value in widths]


def block_of(r, width):
    at = (r * (-(-(1 << 20) // width))) >> 20
    return at, r - at * width


def quad_rows(r):
    return r >> 2, r & 3


def pair_rows(r):
    return (r >> 2) & 1, 4 * (r >> 3) + (r & 3)


def group_rows(pairs):
    def get(r):
        p, local = block_of(r, PAIR_ROWS)
        q, b = pair_rows(local)
        beyond = r >= PAIR_ROWS * pairs
        return jnp.where(beyond, -1, 2 * p + q), jnp.where(beyond, -1, b)

    return get


def field_rows(r):
    k, local = block_of(r, QUAD_ROWS)
    return local >> 2, 4 * k + (local & 3)


def ones_where(cond):
    return jnp.where(cond, 1.0, 0.0)


def dot(a, b):
    return lax.dot_general(a, b, (((1,), (0,)), ((), ())), preferred_element_type=f32)


def dot_t(a, b):
    return lax.dot_general(a, b, (((1,), (1,)), ((), ())), preferred_element_type=f32)


def parts(x, count):
    out = []
    for _ in range(count):
        hi = x.astype(bf16)
        out.append(hi.astype(f32))
        x = x - out[-1]
    return out


def stack_parts(mats, count, pitch):
    pieces = []
    for mat in mats:
        pad = jnp.zeros((pitch - mat.shape[0], mat.shape[1]), f32)
        for part in parts(mat, count):
            pieces += [part, pad]
    return jnp.concatenate(pieces, axis=0).astype(bf16)


def block_matrix(data, pitch, count, layout, row_w, row_blocks, col_w, col_blocks, on_q, triple=False):
    size = data.shape[1]
    mats = data.shape[0] // (pitch * count)
    row_parts = 1 if triple else count
    col_parts = 3 if triple else count
    rows = row_parts * row_blocks * row_w
    cols = col_parts * col_blocks * col_w
    r = lax.broadcasted_iota(jnp.int32, (rows, 1), 0)
    c = lax.broadcasted_iota(jnp.int32, (1, cols), 1)
    row_at, row_local = block_of(r, row_w)
    col_at, col_local = block_of(c, col_w)
    row_q, row_b = layout(row_local)
    col_q, col_b = layout(col_local)
    row_i, row_m = (row_q, row_b) if on_q else (row_b, row_q)
    col_i, col_m = (col_q, col_b) if on_q else (col_b, col_q)
    row_part, row_block = block_of(row_at, row_blocks)
    col_part, col_block = block_of(col_at, col_blocks)
    k = lax.broadcasted_iota(jnp.int32, (size, 1), 0)
    right = ones_where(k == col_i).astype(bf16)
    s = lax.broadcasted_iota(jnp.int32, (1, data.shape[0]), 1)
    mask = row_m == col_m
    if triple:
        s_block, s_local = block_of(s, pitch)
        s_mat = s_block >> 1
        left = ones_where((s_local == row_i) & (s_mat == row_block)).astype(bf16)
        t = lax.broadcasted_iota(jnp.int32, (data.shape[0], 1), 0)
        t_part = block_of(t, pitch)[0] & 1
        wide = dot(data, right)
        wide = jnp.where(t_part == (col_part & 1), wide, 0.0).astype(bf16)
        out = dot(left, wide)
    elif col_blocks == 1:
        left = ones_where(s == (row_block * count + row_part) * pitch + row_i).astype(bf16)
        out = dot(dot(left, data).astype(bf16), right)
        mask = mask & (row_part + col_part < count)
    else:
        s_local = block_of(s, pitch * count)[1]
        left = ones_where(s_local == row_part * pitch + row_i).astype(bf16)
        t = lax.broadcasted_iota(jnp.int32, (data.shape[0], 1), 0)
        wide = dot(data, right)
        wide = jnp.where(block_of(t, pitch * count)[0] == col_block, wide, 0.0).astype(bf16)
        out = dot(left, wide)
        mask = mask & (row_part + col_part < count)
    return jnp.where(mask, out, 0.0).astype(bf16)


def prep_body(
    stiff_ref,
    fm_ref,
    fp_ref,
    jac_ref,
    fluxm_ref,
    fluxp_ref,
    basis_ref,
    rot_ref,
    lq_ref,
    lb_ref,
    jq_ref,
    sp_ref,
    ex_ref,
    ju_ref,
    fa_ref,
    fb_ref,
    jp_ref,
    jq3_ref,
    sp3_ref,
    rb_ref,
    lift_ref,
):
    jac = [jac_ref[x] for x in range(3)]
    minus_stiff = [-stiff_ref[d] for d in range(3)]
    jac_data = stack_parts(jac, 2, 16)
    jq_ref[...] = block_matrix(jac_data, 16, 2, quad_rows, 56, 3, 56, 1, True, True)
    jac_data = stack_parts(jac, 3, 16)
    jq3_ref[...] = block_matrix(jac_data, 16, 3, quad_rows, 56, 3, 56, 1, True)
    for count, ref in ((2, sp_ref), (3, sp3_ref)):
        stiff_data = stack_parts(minus_stiff, count, 24)
        ref[...] = block_matrix(stiff_data, 24, count, pair_rows, 40, 1, 40, 3, False)
    last_data = stack_parts(jac + [-fluxm_ref[...]], 2, 16)
    ju_ref[...] = block_matrix(last_data, 16, 2, quad_rows, 56, 1, 56, 4, True)
    plus_data = stack_parts([-fluxp_ref[...]], 2, 16)
    jp_ref[...] = block_matrix(plus_data, 16, 2, quad_rows, 56, 1, 56, 1, True)
    for f in range(4):
        face_data = stack_parts([fp_ref[:, f, :]], 2, 24)
        fa_ref[f] = block_matrix(face_data, 24, 2, group_rows(2), 80, 1, 128, 1, False)
        fb_ref[f] = block_matrix(face_data, 24, 2, group_rows(3), 120, 1, 128, 1, False)
    expand = [stiff_ref[d].T for d in range(3)] + [fm_ref[:, f, :] for f in range(4)]
    expand_data = stack_parts(expand, 2, 24)
    ex_ref[...] = block_matrix(expand_data, 24, 2, pair_rows, 40, 7, 40, 1, False, True)

    def spread(x, right):
        return sum(dot(part.astype(bf16), right) for part in reversed(parts(x, 3)))

    column = lax.broadcasted_iota(jnp.int32, (1, 3 * ROWS), 1)
    column_part, column = block_of(column, ROWS)
    column_q, column_b = field_rows(column)
    q_id = lax.broadcasted_iota(jnp.int32, (QUANT, 1), 0)
    b_id = lax.broadcasted_iota(jnp.int32, (BASIS, 1), 0)
    rot = spread(rot_ref[...], ones_where(q_id == column_q).astype(bf16))
    bas = spread(basis_ref[...], ones_where(b_id == column_b).astype(bf16))
    full = jnp.concatenate([rot[i : i + 1, :] * bas for i in range(8)], axis=0)
    rows = [jnp.where(column_part < 3 - h, part, 0.0) for h, part in enumerate(parts(full, 3))]
    rb_ref[...] = jnp.concatenate(rows, axis=0).astype(bf16)
    lane = lax.broadcasted_iota(jnp.int32, (1, 256), 1)
    i_id = lax.broadcasted_iota(jnp.int32, (FQUANT, 1), 0)
    k_id = lax.broadcasted_iota(jnp.int32, (POINTS, 1), 0)
    lq = spread(lq_ref[...].T, ones_where(i_id == ((lane >> 4) & 7)).astype(bf16))
    lb = spread(lb_ref[...].T, ones_where(k_id == (lane & 15)).astype(bf16))
    pieces = []
    upper = lax.broadcasted_iota(jnp.int32, (8, 256), 0) < 4
    for k in range(QUADS):
        quad = lb[4 * k : 4 * k + 4, :]
        quad = jnp.concatenate([quad, quad], axis=0)
        for p in range(PAIRS):
            first = lq[2 * p : 2 * p + 1, :]
            second = lq[2 * p + 1 : 2 * p + 2, :] if p < 6 else jnp.zeros_like(first)
            pieces.append(jnp.where(upper, first, second) * quad)
    hi, lo = parts(jnp.concatenate(pieces, axis=0), 2)
    lo = jnp.where(lane < 128, lo, 0.0)
    lift_ref[...] = jnp.concatenate([hi, lo], axis=0).astype(bf16)


PREP_SHAPES = (
    (168, 168),
    (80, 240),
    (280, 120),
    (112, 448),
    (4, 160, 256),
    (4, 240, 256),
    (112, 112),
    (504, 168),
    (120, 360),
    (384, 3 * ROWS),
    (2 * ROWS, 256),
)


def params(**kw):
    return pltpu.CompilerParams(vmem_limit_bytes=VMEM_LIMIT, **kw)


def prep(*matrices):
    return pl.pallas_call(
        prep_body,
        out_shape=[jax.ShapeDtypeStruct(s, bf16) for s in PREP_SHAPES],
        compiler_params=params(),
        name="prep",
    )(*matrices)


def pick(x, tiles):
    return [x[8 * t : 8 * t + 8, :] for t in tiles]


def fold(out, count):
    size = out.shape[0] // count
    total = out[(count - 1) * size :]
    for h in reversed(range(count - 1)):
        total = out[h * size : (h + 1) * size] + total
    return total


def part_product(matrix, blocks, count):
    right = jnp.concatenate([b for part in blocks for b in part], axis=0)
    return fold(dot(matrix, right.astype(bf16)), count)


def quad(x, k):
    return x[QUAD_ROWS * k : QUAD_ROWS * (k + 1)]


def derivative(field, geo, jq, sp, count):
    pieces = parts(field, count)
    blocks = [[], [], []]
    for k in range(QUADS):
        if count == 2:
            hi, lo = quad(pieces[0], k), quad(pieces[1], k)
            out = dot(jq, jnp.concatenate([hi, hi, lo], axis=0).astype(bf16))
        else:
            out = part_product(jq, [[quad(x, k)] for x in pieces], count)
        for d in range(3):
            blocks[d].append(
                geo[3 * d] * quad(out, 0) + geo[3 * d + 1] * quad(out, 1) + geo[3 * d + 2] * quad(out, 2)
            )
    directed = [parts(jnp.concatenate(block, axis=0), count) for block in blocks]
    tiles = [None] * (PAIRS * QUADS)
    for p in range(PAIRS):
        chosen = pair_tiles(p)
        right = []
        for h in range(count):
            right.append([t for d in range(3) for t in pick(directed[d][h], chosen)])
        out = part_product(sp, right, count)
        for k, t in enumerate(chosen):
            tiles[t] = out[8 * k : 8 * k + 8, :]
    return jnp.concatenate(tiles, axis=0)


def load_field(ref):
    tiles = []
    for k in range(QUADS):
        for p in range(PAIRS):
            low = ref[2 * p, 4 * k : 4 * k + 4, :]
            high = ref[2 * p + 1, 4 * k : 4 * k + 4, :] if p < 6 else jnp.zeros_like(low)
            tiles.append(jnp.concatenate([low, high], axis=0))
    return jnp.concatenate(tiles, axis=0)


def copy_rows(sources, table_ref, picked_ref):
    for base in range(0, len(sources), 32):
        got = [
            table_ref[pl.ds(pl.multiple_of(row * 8, 8), 8), :] for row in sources[base : base + 32]
        ]
        for k, value in enumerate(got):
            picked_ref[8 * (base + k) : 8 * (base + k) + 8, :] = value


def send_body(index_ref, coef_ref, geo_ref, out_ref, table_ref, picked_ref):
    elems = coef_ref.shape[2]
    slots = picked_ref.shape[0] // 8
    for c in range(elems // 128):
        cols = pl.ds(128 * c, 128)
        field = load_field(coef_ref.at[:, :, cols])
        geo = [geo_ref[d, x : x + 1, cols] for d in range(3) for x in range(3)]
        geo = jnp.concatenate(geo + [jnp.zeros((384 - ROWS - 9, 128), f32)], axis=0)
        stacked = jnp.concatenate([field, geo], axis=0)
        for j in range(3):
            table_ref[pl.ds(128 * 8 * c + j, 128, stride=8), :] = stacked[128 * j : 128 * (j + 1)].T

    copy_rows(
        [index_ref[s % 8, s // 8] for s in range(slots)], table_ref, picked_ref
    )
    for j in range(3):
        out_ref[:, :, 128 * j : 128 * (j + 1)] = picked_ref[pl.ds(j, slots, stride=8), :].reshape(
            slots // 8, 8, 128
        )


def send(index, coefficients, geometry):
    elems = coefficients.shape[2]
    slots = index.shape[0] * index.shape[1]
    return pl.pallas_call(
        send_body,
        out_shape=jax.ShapeDtypeStruct((slots // 8, 8, 384), f32),
        in_specs=[
            pl.BlockSpec(memory_space=pltpu.SMEM),
            pl.BlockSpec(memory_space=pltpu.VMEM),
            pl.BlockSpec(memory_space=pltpu.VMEM),
        ],
        out_specs=pl.BlockSpec(memory_space=pltpu.VMEM),
        scratch_shapes=[pltpu.VMEM((elems * 8, 128), f32), pltpu.VMEM((slots * 8, 128), f32)],
        compiler_params=params(),
        name="send",
    )(index, coefficients, geometry)


STEP_WEIGHTS = [time_step ** (power + 1) / math.factorial(power + 1) for power in range(ORDER)]


def main_body(
    coef_ref,
    geo_ref,
    scale_ref,
    jq_ref,
    sp_ref,
    ex_ref,
    ju_ref,
    integ_ref,
    part_ref,
    first_ref,
    last_ref,
):
    step = pl.program_id(0)
    field = load_field(coef_ref)
    geo = [geo_ref[d, x : x + 1, :] for d in range(3) for x in range(3)]
    integ_ref[...] = STEP_WEIGHTS[0] * field
    current = field
    for power in range(1, ORDER):
        current = derivative(current, geo, jq_ref[...], sp_ref[...], 2)
        integ_ref[...] += STEP_WEIGHTS[power] * current
    integrated = integ_ref[...]

    @pl.when(step == 0)
    def _():
        first_ref[...] = integrated[:, :GHOST]

    @pl.when(step == pl.num_programs(0) - 1)
    def _():
        last_ref[...] = integrated[:, integrated.shape[1] - GHOST :]

    hi, lo = parts(integrated, 2)
    pieces = [[None] * (PAIRS * QUADS) for _ in range(4)]
    scale = [scale_ref[f : f + 1, :] for f in range(4)]
    for p in range(PAIRS):
        chosen = pair_tiles(p)
        right = pick(hi, chosen) + pick(hi, chosen) + pick(lo, chosen)
        out = dot(ex_ref[...], jnp.concatenate(right, axis=0).astype(bf16))
        blocks = [out[PAIR_ROWS * k : PAIR_ROWS * (k + 1)] for k in range(7)]
        results = [
            geo[x] * blocks[0] + geo[3 + x] * blocks[1] + geo[6 + x] * blocks[2] for x in range(3)
        ]
        results.append(
            scale[0] * blocks[3] + scale[1] * blocks[4] + scale[2] * blocks[5] + scale[3] * blocks[6]
        )
        for m in range(4):
            for k, t in enumerate(chosen):
                pieces[m][t] = results[m][8 * k : 8 * k + 8]
    pairs = [parts(jnp.concatenate(tiles, axis=0), 2) for tiles in pieces]
    for k in range(QUADS):
        out = part_product(ju_ref[...], [[quad(pair[h], k) for pair in pairs] for h in range(2)], 2)
        rows = slice(QUAD_ROWS * k, QUAD_ROWS * (k + 1))
        part_ref[rows, :] = field[rows] + out


def whole(array):
    shape = array.shape
    return pl.BlockSpec(shape, lambda *_: (0,) * len(shape))


def main(coefficients, geometry, face_scale, mats):
    elems = coefficients.shape[2]
    block = pl.BlockSpec((ROWS, MAIN_COLS), lambda i: (0, i))
    fixed = pl.BlockSpec((ROWS, GHOST), lambda i: (0, 0))
    field = jax.ShapeDtypeStruct((ROWS, elems), f32)
    rim = jax.ShapeDtypeStruct((ROWS, GHOST), f32)
    return pl.pallas_call(
        main_body,
        grid=(elems // MAIN_COLS,),
        out_shape=[field, field, rim, rim],
        in_specs=[
            pl.BlockSpec((QUANT, BASIS, MAIN_COLS), lambda i: (0, 0, i)),
            pl.BlockSpec((3, 3, MAIN_COLS), lambda i: (0, 0, i)),
            pl.BlockSpec((FACES, MAIN_COLS), lambda i: (0, i)),
        ]
        + [whole(m) for m in mats],
        out_specs=[block, block, fixed, fixed],
        compiler_params=params(),
        name="main",
    )(coefficients, geometry, face_scale, *mats)


def inverse_sinh(value):
    magnitude = jnp.abs(value)
    result = jnp.log(magnitude + jnp.sqrt(magnitude * magnitude + 1.0))
    return jnp.where(value < 0.0, -result, result)


def friction(minus, plus, ns, ss, pp, rate, state, direct, evolution, slip, widths):
    damping = 0.5 * impedance_shear
    slip_rate = rate
    state_now = state
    back = [[0.0] * 8, [0.0] * 8]
    for j in range(TPOINTS):
        m = [minus(i, j) for i in range(8)]
        n = [plus(i, j) for i in range(8)]
        normal_mid = 0.5 * (m[0] + n[0]) + 0.5 * impedance_normal * (n[3] - m[3])
        shear_one = 0.5 * (m[1] + n[1]) + 0.5 * impedance_shear * (n[4] - m[4])
        shear_two = 0.5 * (m[2] + n[2]) + 0.5 * impedance_shear * (n[5] - m[5])
        fluid_mid = 0.5 * (m[6] + n[6]) + 0.5 * impedance_fluid * (n[7] - m[7])
        effective = jnp.maximum(-(ns + normal_mid + pp + fluid_mid), 0.0)
        total_one = ss[0] + shear_one
        total_two = ss[1] + shear_two
        locked = jnp.sqrt(total_one * total_one + total_two * total_two + 1.0)
        scaled = 0.5 * jnp.exp(state_now / direct)
        floor_term = 4.0 * jnp.exp(-2.0 * state_now / direct)
        strength_rate = effective * direct
        for sweep in range(NEWTON):
            residual = strength_rate * inverse_sinh(scaled * slip_rate) + damping * slip_rate - locked
            slope = strength_rate / jnp.sqrt(floor_term + slip_rate * slip_rate) + damping
            slip_rate = slip_rate - residual / slope
        steady = friction_ref - (evolution - direct) * 0.5 * jnp.log(
            slip_rate * slip_rate + rate_floor
        )
        state_now = steady + (state_now - steady) * jnp.exp(-jnp.abs(slip_rate) * widths[j] / slip)
        strength = locked - damping * slip_rate
        traction_one = strength * total_one / locked - ss[0]
        traction_two = strength * total_two / locked - ss[1]
        h = widths[j]
        for side, t, sign in ((0, m, 1.0), (1, n, -1.0)):
            d0 = normal_mid - t[0]
            d1 = traction_one - t[1]
            d2 = traction_two - t[2]
            d6 = fluid_mid - t[6]
            changes = [
                d0,
                d1,
                d2,
                d0 * (sign / impedance_normal),
                d1 * (sign / impedance_shear),
                d2 * (sign / impedance_shear),
                d6,
                d6 * (sign / impedance_fluid),
            ]
            for i in range(8):
                back[side][i] = back[side][i] + h * changes[i]
    return slip_rate, state_now, back[0], back[1]


def fault_body(
    minus_ref,
    plus_ref,
    arr_ref,
    jq_ref,
    sp_ref,
    rb_ref,
    ns_ref,
    ss_ref,
    pp_ref,
    rate_ref,
    state_ref,
    direct_ref,
    evol_ref,
    slip_ref,
    ret_ref,
    rate_out,
    state_out,
    table_ref,
    picked_ref,
    trace_ref,
    rows_ref,
):
    slots = table_ref.shape[0] // 8
    sides = picked_ref.shape[0] // 8
    faces = sides // 2
    for j in range(3):
        table_ref[pl.ds(j, slots, stride=8), :] = arr_ref[:, :, 128 * j : 128 * (j + 1)].reshape(
            slots, 128
        )

    slot_ids = [ref[s] for ref in (minus_ref, plus_ref) for s in range(faces)]
    copy_rows(slot_ids, table_ref, picked_ref)
    taylor, widths = time_tables()
    columns = []
    for c in range(sides // 128):
        columns.append(
            jnp.concatenate(
                [picked_ref[pl.ds(1024 * c + j, 128, stride=8), :].T for j in range(3)], axis=0
            )
        )
    stacked = jnp.concatenate(columns, axis=1)
    current = stacked[:ROWS]
    geo = [stacked[ROWS + k : ROWS + k + 1] for k in range(9)]
    for m in range(ORDER):
        if m > 0:
            current = derivative(current, geo, jq_ref[...], sp_ref[...], 3)
        trace_ref[m] = part_product(rb_ref[...], [[x] for x in parts(current, 3)], 3)

    def trace_of(side):
        def get(i, j):
            cols = slice(side * faces, (side + 1) * faces)
            value = trace_ref[0, 16 * i : 16 * i + 16, cols] * taylor[j][0]
            for m in range(1, ORDER):
                value = value + taylor[j][m] * trace_ref[m, 16 * i : 16 * i + 16, cols]
            return value

        return get

    slip_rate, state_now, back_minus, back_plus = friction(
        trace_of(0),
        trace_of(1),
        ns_ref[...],
        (ss_ref[0], ss_ref[1]),
        pp_ref[...],
        rate_ref[...],
        state_ref[...],
        direct_ref[...],
        evol_ref[...],
        slip_ref[...],
        widths,
    )
    rate_out[...] = slip_rate
    state_out[...] = state_now
    for side, back in ((0, back_minus), (1, back_plus)):
        stacked = jnp.concatenate(back, axis=0)
        for c in range(faces // 128):
            rows_ref[pl.ds(side * faces + 128 * c, 128), :] = stacked[:, 128 * c : 128 * (c + 1)].T
    ret_ref[...] = jnp.zeros_like(ret_ref)

    for s in range(sides):
        ret_ref[pl.ds(slot_ids[s], 1), :] = rows_ref[s : s + 1, :]


def fault(minus_slot, plus_slot, arrived, mats, fields):
    slots = arrived.shape[0] * arrived.shape[1]
    faces = minus_slot.shape[0]
    sides = 2 * faces
    point = jax.ShapeDtypeStruct((POINTS, faces), f32)
    vmem = pl.BlockSpec(memory_space=pltpu.VMEM)
    return pl.pallas_call(
        fault_body,
        out_shape=[jax.ShapeDtypeStruct((slots, 128), f32), point, point],
        in_specs=[pl.BlockSpec(memory_space=pltpu.SMEM)] * 2 + [vmem] * (1 + len(mats) + len(fields)),
        out_specs=[vmem] * 3,
        scratch_shapes=[
            pltpu.VMEM((slots * 8, 128), f32),
            pltpu.VMEM((sides * 8, 128), f32),
            pltpu.VMEM((ORDER, 128, sides), f32),
            pltpu.VMEM((sides, 128), f32),
        ],
        compiler_params=params(),
        name="fault",
    )(minus_slot, plus_slot, arrived, *mats, *fields)


def beside_body(
    index_ref,
    integ_ref,
    low_ref,
    high_ref,
    part_ref,
    scale_ref,
    fa_ref,
    fb_ref,
    jp_ref,
    out_ref,
    table_ref,
    picked_ref,
):
    step = pl.program_id(0)
    elems = integ_ref.shape[1]

    @pl.when(step == 0)
    def _():
        for source, first, count in (
            (low_ref, 0, GHOST),
            (integ_ref, GHOST, elems),
            (high_ref, GHOST + elems, GHOST),
        ):
            for c in range(count // 128):
                field = source[:, 128 * c : 128 * (c + 1)]
                for j, tiles in enumerate(GROUPS):
                    rows = pick(field, tiles)
                    pad = 128 - 8 * len(tiles)
                    stacked = jnp.concatenate(rows + [jnp.zeros((pad, 128), f32)], axis=0)
                    table_ref[pl.ds(8 * (first + 128 * c) + j, 128, stride=8), :] = stacked.T
        table_ref[pl.ds(8 * (elems + 2 * GHOST), 8), :] = jnp.zeros((8, 128), f32)

    scale = [scale_ref[f : f + 1, :] for f in range(4)]
    total = [None] * (PAIRS * QUADS)
    for f in range(FACES):
        copy_rows([index_ref[f, s] for s in range(COLS)], table_ref, picked_ref)
        for j, tiles in enumerate(GROUPS):
            hi, lo = parts(picked_ref[pl.ds(j, COLS, stride=8), :], 2)
            right = jnp.concatenate([hi, lo], axis=1).astype(bf16)
            out = dot_t(fb_ref[f] if j == 2 else fa_ref[f], right)
            half = out.shape[0] // 2
            out = scale[f] * (out[:half] + out[half:])
            for k, t in enumerate(tiles):
                value = out[8 * k : 8 * k + 8]
                total[t] = value if total[t] is None else total[t] + value
    hi, lo = parts(jnp.concatenate(total, axis=0), 2)
    for k in range(QUADS):
        out = part_product(jp_ref[...], [[quad(hi, k)], [quad(lo, k)]], 2)
        rows = slice(QUAD_ROWS * k, QUAD_ROWS * (k + 1))
        out_ref[rows, :] = part_ref[rows, :] + out


def beside(neighbours, integrated, low, high, partial, face_scale, mats):
    elems = integrated.shape[1]
    block = pl.BlockSpec((ROWS, COLS), lambda i: (0, i))
    return pl.pallas_call(
        beside_body,
        grid=(elems // COLS,),
        out_shape=jax.ShapeDtypeStruct((ROWS, elems), f32),
        in_specs=[
            pl.BlockSpec((FACES, COLS), lambda i: (0, i), memory_space=pltpu.SMEM),
            whole(integrated),
            whole(low),
            whole(high),
            block,
            pl.BlockSpec((FACES, COLS), lambda i: (0, i)),
        ]
        + [whole(m) for m in mats],
        out_specs=block,
        scratch_shapes=[
            pltpu.VMEM(((elems + 2 * GHOST + 8) * 8, 128), f32),
            pltpu.VMEM((COLS * 8, 128), f32),
        ],
        compiler_params=params(),
        name="beside",
    )(neighbours, integrated, low, high, partial, face_scale, *mats)


def lift_body(elem_ref, back_ref, part_ref, scale_ref, lift_ref, out_ref):
    step = pl.program_id(0)
    cols = out_ref.shape[2]
    capacity, owners = elem_ref.shape
    values, chosen = [], []
    ids = lax.broadcasted_iota(jnp.int32, (cols, owners), 0) + step * cols
    for c in range(capacity):
        hi, lo = parts(back_ref[pl.ds(c, owners, stride=capacity), :], 2)
        values.append(jnp.concatenate([hi, lo], axis=1).astype(bf16))
        chosen.append(ones_where(ids == elem_ref[c : c + 1, :]).astype(bf16))
    summed = dot(jnp.concatenate(chosen, axis=1), jnp.concatenate(values, axis=0))
    hi, lo = parts(summed[:, :128] + summed[:, 128:], 2)
    out = dot_t(lift_ref[...], jnp.concatenate([hi, lo], axis=1).astype(bf16))
    out = part_ref[...] + scale_ref[FACES - 1 : FACES, :] * (out[:ROWS] + out[ROWS:])
    for q in range(13):
        for k in range(QUADS):
            at = QUAD_ROWS * k + 4 * q
            out_ref[q, 4 * k : 4 * k + 4, :] = out[at : at + 4]


def lift(elem_row, back, partial, face_scale, matrix):
    elems = partial.shape[1]
    cols = 512
    return pl.pallas_call(
        lift_body,
        grid=(elems // cols,),
        out_shape=jax.ShapeDtypeStruct((QUANT, BASIS, elems), f32),
        in_specs=[
            whole(elem_row),
            whole(back),
            pl.BlockSpec((ROWS, cols), lambda i: (0, i)),
            pl.BlockSpec((FACES, cols), lambda i: (0, i)),
            whole(matrix),
        ],
        out_specs=pl.BlockSpec((QUANT, BASIS, cols), lambda i: (0, 0, i)),
        compiler_params=params(),
        name="lift",
    )(elem_row, back, partial, face_scale, matrix)


def shards(
    coefficients,
    geometry,
    face_scale,
    neighbours,
    stiffness,
    face_minus,
    face_plus,
    jacobians,
    flux_minus,
    flux_plus,
    face_basis,
    rotation,
    lift_quantity,
    lift_basis,
    send_elements,
    send_count,
    minus_slot,
    plus_slot,
    normal_stress,
    shear_stress,
    pore_pressure,
    initial_rate,
    initial_state,
    direct_effect,
    evolution_effect,
    slip_length,
):
    part_count = send_elements.shape[1]
    capacity = send_elements.shape[2]
    slot_total = part_count * capacity
    slot_elements = jnp.transpose(send_elements[0])
    outgoing = send(slot_elements, coefficients, geometry)
    arrived = lax.all_to_all(outgoing, AXES, split_axis=0, concat_axis=0, tiled=True)
    mats = prep(
        stiffness,
        jnp.transpose(face_minus, (1, 0, 2)),
        jnp.transpose(face_plus, (1, 0, 2)),
        jacobians,
        flux_minus,
        flux_plus,
        face_basis,
        rotation,
        lift_quantity.T,
        lift_basis.T,
    )
    jq, sp, ex, ju, fa, fb, jp, jq3, sp3, rb, lift_matrix = mats
    integrated, partial, first, last = main(
        coefficients, geometry, face_scale, (jq, sp, ex, ju)
    )
    arrived, first, last = lax.optimization_barrier((arrived, first, last))
    count = part_count
    forward = [(i, i + 1) for i in range(count - 1)]
    backward = [(target, source) for source, target in forward]
    low = lax.ppermute(last, AXES, forward)
    high = lax.ppermute(first, AXES, backward)
    returned, slip_rate, fault_state = fault(
        minus_slot,
        plus_slot,
        arrived,
        (jq3, sp3, rb),
        (
            normal_stress,
            shear_stress,
            pore_pressure,
            initial_rate,
            initial_state,
            direct_effect,
            evolution_effect,
            slip_length,
        ),
    )
    returned, low, high = lax.optimization_barrier((returned, low, high))
    back = lax.all_to_all(
        returned.reshape(part_count, capacity, 128), AXES, split_axis=0, concat_axis=0, tiled=True
    )
    partial = beside(neighbours, integrated, low, high, partial, face_scale, (fa, fb, jp))
    updated = lift(
        slot_elements,
        back.reshape(slot_total, 128),
        partial,
        face_scale,
        lift_matrix,
    )
    return (updated, slip_rate, fault_state)


def solution(mesh):
    cols = P(None, AXES)
    in_specs = (
        P(None, None, AXES),
        P(None, None, AXES),
        cols,
        cols,
        *(P() for _ in range(10)),
        P(AXES, None, None),
        P(AXES, None),
        P(AXES),
        P(AXES),
        cols,
        P(None, None, AXES),
        *(cols for _ in range(6)),
    )
    out_specs = (P(None, None, AXES), cols, cols)
    return jax.shard_map(shards, mesh=mesh, in_specs=in_specs, out_specs=out_specs, check_vma=False)
```

```python
import math

import jax
import jax.numpy as jnp
import numpy as np
from jax import lax
from jax.experimental import pallas as pl
from jax.experimental.pallas import tpu as pltpu
from jax.sharding import PartitionSpec as P

QUANT = 13
BASIS = 20
ORDER = 4
FACES = 4
POINTS = 16
TPOINTS = 4
FQUANT = 8
NEWTON = 6
GHOST = 256
COLS = 512
MAIN_COLS = 1024

time_step = 0.5
friction_ref = 0.6
impedance_normal = 2.0
impedance_shear = 1.2
impedance_fluid = 0.8
rate_floor = 0.01
gauss_inner = 0.3399810435848563
gauss_outer = 0.8611363115940526
weight_inner = 0.6521451548625461
weight_outer = 0.3478548451374538

f32 = jnp.float32
bf16 = jnp.bfloat16
AXES = ("space", "sub")
VMEM_LIMIT = 56 * 1024 * 1024

QUADS = 5
PAIRS = 7
ROWS = 280
QUAD_ROWS = 56
PAIR_ROWS = 40


def pair_tiles(p):
    return [PAIRS * k + p for k in range(QUADS)]


GROUPS = tuple([t for p in pairs for t in pair_tiles(p)] for pairs in ((0, 1), (2, 3), (4, 5, 6)))


def time_tables():
    gauss_nodes = [-gauss_outer, -gauss_inner, gauss_inner, gauss_outer]
    gauss_weights = [weight_outer, weight_inner, weight_inner, weight_outer]
    time_points = [time_step * (1.0 + node_value) / 2.0 for node_value in gauss_nodes]
    widths = [time_step * weight_value / 2.0 for weight_value in gauss_weights]
    taylor = [
        [float(np.float32(point_value**power / math.factorial(power))) for power in range(ORDER)]
        for point_value in time_points
    ]
    return taylor, [float(width_value) for width_value in widths]


def block_of(r, width):
    at = (r * (-(-(1 << 20) // width))) >> 20
    return at, r - at * width


def quad_rows(r):
    return r >> 2, r & 3


def pair_rows(r):
    return (r >> 2) & 1, 4 * (r >> 3) + (r & 3)


def group_rows(pairs):
    def get(r):
        p, local = block_of(r, PAIR_ROWS)
        q, b = pair_rows(local)
        beyond = r >= PAIR_ROWS * pairs
        return jnp.where(beyond, -1, 2 * p + q), jnp.where(beyond, -1, b)

    return get


def field_rows(r):
    k, local = block_of(r, QUAD_ROWS)
    return local >> 2, 4 * k + (local & 3)


def ones_where(cond):
    return jnp.where(cond, 1.0, 0.0)


def dot(a, b):
    return lax.dot_general(a, b, (((1,), (0,)), ((), ())), preferred_element_type=f32)


def dot_t(a, b):
    return lax.dot_general(a, b, (((1,), (1,)), ((), ())), preferred_element_type=f32)


def parts(x, count):
    out = []
    for _ in range(count):
        hi = x.astype(bf16)
        out.append(hi.astype(f32))
        x = x - out[-1]
    return out


def stack_parts(mats, count, pitch):
    pieces = []
    for mat in mats:
        pad = jnp.zeros((pitch - mat.shape[0], mat.shape[1]), f32)
        for part in parts(mat, count):
            pieces += [part, pad]
    return jnp.concatenate(pieces, axis=0).astype(bf16)


def block_matrix(data, pitch, count, layout, row_w, row_blocks, col_w, col_blocks, on_q, triple=False):
    size = data.shape[1]
    mats = data.shape[0] // (pitch * count)
    row_parts = 1 if triple else count
    col_parts = 3 if triple else count
    rows = row_parts * row_blocks * row_w
    cols = col_parts * col_blocks * col_w
    r = lax.broadcasted_iota(jnp.int32, (rows, 1), 0)
    c = lax.broadcasted_iota(jnp.int32, (1, cols), 1)
    row_at, row_local = block_of(r, row_w)
    col_at, col_local = block_of(c, col_w)
    row_q, row_b = layout(row_local)
    col_q, col_b = layout(col_local)
    row_i, row_m = (row_q, row_b) if on_q else (row_b, row_q)
    col_i, col_m = (col_q, col_b) if on_q else (col_b, col_q)
    row_part, row_block = block_of(row_at, row_blocks)
    col_part, col_block = block_of(col_at, col_blocks)
    k = lax.broadcasted_iota(jnp.int32, (size, 1), 0)
    right = ones_where(k == col_i).astype(bf16)
    s = lax.broadcasted_iota(jnp.int32, (1, data.shape[0]), 1)
    mask = row_m == col_m
    if triple:
        s_block, s_local = block_of(s, pitch)
        s_mat = s_block >> 1
        left = ones_where((s_local == row_i) & (s_mat == row_block)).astype(bf16)
        t = lax.broadcasted_iota(jnp.int32, (data.shape[0], 1), 0)
        t_part = block_of(t, pitch)[0] & 1
        wide = dot(data, right)
        wide = jnp.where(t_part == (col_part & 1), wide, 0.0).astype(bf16)
        out = dot(left, wide)
    elif col_blocks == 1:
        left = ones_where(s == (row_block * count + row_part) * pitch + row_i).astype(bf16)
        out = dot(dot(left, data).astype(bf16), right)
        mask = mask & (row_part + col_part < count)
    else:
        s_local = block_of(s, pitch * count)[1]
        left = ones_where(s_local == row_part * pitch + row_i).astype(bf16)
        t = lax.broadcasted_iota(jnp.int32, (data.shape[0], 1), 0)
        wide = dot(data, right)
        wide = jnp.where(block_of(t, pitch * count)[0] == col_block, wide, 0.0).astype(bf16)
        out = dot(left, wide)
        mask = mask & (row_part + col_part < count)
    return jnp.where(mask, out, 0.0).astype(bf16)


def prep_body(
    stiff_ref,
    fm_ref,
    fp_ref,
    jac_ref,
    fluxm_ref,
    fluxp_ref,
    basis_ref,
    rot_ref,
    lq_ref,
    lb_ref,
    jq_ref,
    sp_ref,
    ex_ref,
    ju_ref,
    fa_ref,
    fb_ref,
    jp_ref,
    jq3_ref,
    sp3_ref,
    rb_ref,
    lift_ref,
):
    jac = [jac_ref[x] for x in range(3)]
    minus_stiff = [-stiff_ref[d] for d in range(3)]
    jac_data = stack_parts(jac, 2, 16)
    jq_ref[...] = block_matrix(jac_data, 16, 2, quad_rows, 56, 3, 56, 1, True, True)
    jac_data = stack_parts(jac, 3, 16)
    jq3_ref[...] = block_matrix(jac_data, 16, 3, quad_rows, 56, 3, 56, 1, True)
    for count, ref in ((2, sp_ref), (3, sp3_ref)):
        stiff_data = stack_parts(minus_stiff, count, 24)
        ref[...] = block_matrix(stiff_data, 24, count, pair_rows, 40, 1, 40, 3, False)
    last_data = stack_parts(jac + [-fluxm_ref[...]], 2, 16)
    ju_ref[...] = block_matrix(last_data, 16, 2, quad_rows, 56, 1, 56, 4, True)
    plus_data = stack_parts([-fluxp_ref[...]], 2, 16)
    jp_ref[...] = block_matrix(plus_data, 16, 2, quad_rows, 56, 1, 56, 1, True)
    for f in range(4):
        face_data = stack_parts([fp_ref[:, f, :]], 2, 24)
        fa_ref[f] = block_matrix(face_data, 24, 2, group_rows(2), 80, 1, 128, 1, False)
        fb_ref[f] = block_matrix(face_data, 24, 2, group_rows(3), 120, 1, 128, 1, False)
    expand = [stiff_ref[d].T for d in range(3)] + [fm_ref[:, f, :] for f in range(4)]
    expand_data = stack_parts(expand, 2, 24)
    ex_ref[...] = block_matrix(expand_data, 24, 2, pair_rows, 40, 7, 40, 1, False, True)

    def spread(x, right):
        return sum(dot(part.astype(bf16), right) for part in reversed(parts(x, 3)))

    column = lax.broadcasted_iota(jnp.int32, (1, 3 * ROWS), 1)
    column_part, column = block_of(column, ROWS)
    column_q, column_b = field_rows(column)
    q_id = lax.broadcasted_iota(jnp.int32, (QUANT, 1), 0)
    b_id = lax.broadcasted_iota(jnp.int32, (BASIS, 1), 0)
    rot = spread(rot_ref[...], ones_where(q_id == column_q).astype(bf16))
    bas = spread(basis_ref[...], ones_where(b_id == column_b).astype(bf16))
    full = jnp.concatenate([rot[i : i + 1, :] * bas for i in range(8)], axis=0)
    rows = [jnp.where(column_part < 3 - h, part, 0.0) for h, part in enumerate(parts(full, 3))]
    rb_ref[...] = jnp.concatenate(rows, axis=0).astype(bf16)
    lane = lax.broadcasted_iota(jnp.int32, (1, 256), 1)
    i_id = lax.broadcasted_iota(jnp.int32, (FQUANT, 1), 0)
    k_id = lax.broadcasted_iota(jnp.int32, (POINTS, 1), 0)
    lq = spread(lq_ref[...].T, ones_where(i_id == ((lane >> 4) & 7)).astype(bf16))
    lb = spread(lb_ref[...].T, ones_where(k_id == (lane & 15)).astype(bf16))
    pieces = []
    upper = lax.broadcasted_iota(jnp.int32, (8, 256), 0) < 4
    for k in range(QUADS):
        quad = lb[4 * k : 4 * k + 4, :]
        quad = jnp.concatenate([quad, quad], axis=0)
        for p in range(PAIRS):
            first = lq[2 * p : 2 * p + 1, :]
            second = lq[2 * p + 1 : 2 * p + 2, :] if p < 6 else jnp.zeros_like(first)
            pieces.append(jnp.where(upper, first, second) * quad)
    hi, lo = parts(jnp.concatenate(pieces, axis=0), 2)
    lo = jnp.where(lane < 128, lo, 0.0)
    lift_ref[...] = jnp.concatenate([hi, lo], axis=0).astype(bf16)


PREP_SHAPES = (
    (168, 168),
    (80, 240),
    (280, 120),
    (112, 448),
    (4, 160, 256),
    (4, 240, 256),
    (112, 112),
    (504, 168),
    (120, 360),
    (384, 3 * ROWS),
    (2 * ROWS, 256),
)


def params(**kw):
    return pltpu.CompilerParams(vmem_limit_bytes=VMEM_LIMIT, **kw)


def prep(*matrices):
    return pl.pallas_call(
        prep_body,
        out_shape=[jax.ShapeDtypeStruct(s, bf16) for s in PREP_SHAPES],
        compiler_params=params(),
        name="prep",
    )(*matrices)


def pick(x, tiles):
    return [x[8 * t : 8 * t + 8, :] for t in tiles]


def fold(out, count):
    size = out.shape[0] // count
    total = out[(count - 1) * size :]
    for h in reversed(range(count - 1)):
        total = out[h * size : (h + 1) * size] + total
    return total


def part_product(matrix, blocks, count):
    right = jnp.concatenate([b for part in blocks for b in part], axis=0)
    return fold(dot(matrix, right.astype(bf16)), count)


def quad(x, k):
    return x[QUAD_ROWS * k : QUAD_ROWS * (k + 1)]


def derivative(field, geo, jq, sp, count):
    pieces = parts(field, count)
    blocks = [[], [], []]
    for k in range(QUADS):
        if count == 2:
            hi, lo = quad(pieces[0], k), quad(pieces[1], k)
            out = dot(jq, jnp.concatenate([hi, hi, lo], axis=0).astype(bf16))
        else:
            out = part_product(jq, [[quad(x, k)] for x in pieces], count)
        for d in range(3):
            blocks[d].append(
                geo[3 * d] * quad(out, 0) + geo[3 * d + 1] * quad(out, 1) + geo[3 * d + 2] * quad(out, 2)
            )
    directed = [parts(jnp.concatenate(block, axis=0), count) for block in blocks]
    tiles = [None] * (PAIRS * QUADS)
    for p in range(PAIRS):
        chosen = pair_tiles(p)
        right = []
        for h in range(count):
            right.append([t for d in range(3) for t in pick(directed[d][h], chosen)])
        out = part_product(sp, right, count)
        for k, t in enumerate(chosen):
            tiles[t] = out[8 * k : 8 * k + 8, :]
    return jnp.concatenate(tiles, axis=0)


def load_field(ref):
    tiles = []
    for k in range(QUADS):
        for p in range(PAIRS):
            low = ref[2 * p, 4 * k : 4 * k + 4, :]
            high = ref[2 * p + 1, 4 * k : 4 * k + 4, :] if p < 6 else jnp.zeros_like(low)
            tiles.append(jnp.concatenate([low, high], axis=0))
    return jnp.concatenate(tiles, axis=0)


def copy_rows(sources, table_ref, picked_ref):
    for base in range(0, len(sources), 32):
        got = [
            table_ref[pl.ds(pl.multiple_of(row, 8), 8), :] for row in sources[base : base + 32]
        ]
        for k, value in enumerate(got):
            picked_ref[8 * (base + k) : 8 * (base + k) + 8, :] = value


def send_body(index_ref, coef_ref, geo_ref, out_ref, table_ref, picked_ref):
    elems = coef_ref.shape[2]
    slots = picked_ref.shape[0] // 8
    for c in range(elems // 128):
        cols = pl.ds(128 * c, 128)
        field = load_field(coef_ref.at[:, :, cols])
        geo = [geo_ref[d, x : x + 1, cols] for d in range(3) for x in range(3)]
        geo = jnp.concatenate(geo + [jnp.zeros((384 - ROWS - 9, 128), f32)], axis=0)
        stacked = jnp.concatenate([field, geo], axis=0)
        for j in range(3):
            table_ref[pl.ds(128 * 8 * c + j, 128, stride=8), :] = stacked[128 * j : 128 * (j + 1)].T

    copy_rows(
        [index_ref[s % 8, s // 8] * 8 for s in range(slots)], table_ref, picked_ref
    )
    for j in range(3):
        out_ref[:, :, 128 * j : 128 * (j + 1)] = picked_ref[pl.ds(j, slots, stride=8), :].reshape(
            slots // 8, 8, 128
        )


def send(index, coefficients, geometry):
    elems = coefficients.shape[2]
    slots = index.shape[0] * index.shape[1]
    return pl.pallas_call(
        send_body,
        out_shape=jax.ShapeDtypeStruct((slots // 8, 8, 384), f32),
        in_specs=[
            pl.BlockSpec(memory_space=pltpu.SMEM),
            pl.BlockSpec(memory_space=pltpu.VMEM),
            pl.BlockSpec(memory_space=pltpu.VMEM),
        ],
        out_specs=pl.BlockSpec(memory_space=pltpu.VMEM),
        scratch_shapes=[pltpu.VMEM((elems * 8, 128), f32), pltpu.VMEM((slots * 8, 128), f32)],
        compiler_params=params(),
        name="send",
    )(index, coefficients, geometry)


STEP_WEIGHTS = [time_step ** (power + 1) / math.factorial(power + 1) for power in range(ORDER)]


def main_body(
    coef_ref,
    geo_ref,
    scale_ref,
    beside_ref,
    jq_ref,
    sp_ref,
    ex_ref,
    ju_ref,
    integ_ref,
    part_ref,
    first_ref,
    last_ref,
    row_ref,
):
    step = pl.program_id(0)
    row_ref[...] = beside_ref[...] * 8
    field = load_field(coef_ref)
    geo = [geo_ref[d, x : x + 1, :] for d in range(3) for x in range(3)]
    integ_ref[...] = STEP_WEIGHTS[0] * field
    current = field
    for power in range(1, ORDER):
        current = derivative(current, geo, jq_ref[...], sp_ref[...], 2)
        integ_ref[...] += STEP_WEIGHTS[power] * current
    integrated = integ_ref[...]

    @pl.when(step == 0)
    def _():
        first_ref[...] = integrated[:, :GHOST]

    @pl.when(step == pl.num_programs(0) - 1)
    def _():
        last_ref[...] = integrated[:, integrated.shape[1] - GHOST :]

    hi, lo = parts(integrated, 2)
    pieces = [[None] * (PAIRS * QUADS) for _ in range(4)]
    scale = [scale_ref[f : f + 1, :] for f in range(4)]
    for p in range(PAIRS):
        chosen = pair_tiles(p)
        right = pick(hi, chosen) + pick(hi, chosen) + pick(lo, chosen)
        out = dot(ex_ref[...], jnp.concatenate(right, axis=0).astype(bf16))
        blocks = [out[PAIR_ROWS * k : PAIR_ROWS * (k + 1)] for k in range(7)]
        results = [
            geo[x] * blocks[0] + geo[3 + x] * blocks[1] + geo[6 + x] * blocks[2] for x in range(3)
        ]
        results.append(
            scale[0] * blocks[3] + scale[1] * blocks[4] + scale[2] * blocks[5] + scale[3] * blocks[6]
        )
        for m in range(4):
            for k, t in enumerate(chosen):
                pieces[m][t] = results[m][8 * k : 8 * k + 8]
    pairs = [parts(jnp.concatenate(tiles, axis=0), 2) for tiles in pieces]
    for k in range(QUADS):
        out = part_product(ju_ref[...], [[quad(pair[h], k) for pair in pairs] for h in range(2)], 2)
        rows = slice(QUAD_ROWS * k, QUAD_ROWS * (k + 1))
        part_ref[rows, :] = field[rows] + out


def whole(array):
    shape = array.shape
    return pl.BlockSpec(shape, lambda *_: (0,) * len(shape))


def main(coefficients, geometry, face_scale, neighbours, mats):
    elems = coefficients.shape[2]
    block = pl.BlockSpec((ROWS, MAIN_COLS), lambda i: (0, i))
    fixed = pl.BlockSpec((ROWS, GHOST), lambda i: (0, 0))
    field = jax.ShapeDtypeStruct((ROWS, elems), f32)
    rim = jax.ShapeDtypeStruct((ROWS, GHOST), f32)
    return pl.pallas_call(
        main_body,
        grid=(elems // MAIN_COLS,),
        out_shape=[field, field, rim, rim, jax.ShapeDtypeStruct(neighbours.shape, jnp.int32)],
        in_specs=[
            pl.BlockSpec((QUANT, BASIS, MAIN_COLS), lambda i: (0, 0, i)),
            pl.BlockSpec((3, 3, MAIN_COLS), lambda i: (0, 0, i)),
            pl.BlockSpec((FACES, MAIN_COLS), lambda i: (0, i)),
            pl.BlockSpec((FACES, MAIN_COLS), lambda i: (0, i)),
        ]
        + [whole(m) for m in mats],
        out_specs=[
            block,
            block,
            fixed,
            fixed,
            pl.BlockSpec((FACES, MAIN_COLS), lambda i: (0, i)),
        ],
        compiler_params=params(),
        name="main",
    )(coefficients, geometry, face_scale, neighbours, *mats)


def inverse_sinh(value):
    magnitude = jnp.abs(value)
    result = jnp.log(magnitude + jnp.sqrt(magnitude * magnitude + 1.0))
    return jnp.where(value < 0.0, -result, result)


def friction(minus, plus, ns, ss, pp, rate, state, direct, evolution, slip, widths):
    damping = 0.5 * impedance_shear
    slip_rate = rate
    state_now = state
    back = [[0.0] * 8, [0.0] * 8]
    for j in range(TPOINTS):
        m = [minus(i, j) for i in range(8)]
        n = [plus(i, j) for i in range(8)]
        normal_mid = 0.5 * (m[0] + n[0]) + 0.5 * impedance_normal * (n[3] - m[3])
        shear_one = 0.5 * (m[1] + n[1]) + 0.5 * impedance_shear * (n[4] - m[4])
        shear_two = 0.5 * (m[2] + n[2]) + 0.5 * impedance_shear * (n[5] - m[5])
        fluid_mid = 0.5 * (m[6] + n[6]) + 0.5 * impedance_fluid * (n[7] - m[7])
        effective = jnp.maximum(-(ns + normal_mid + pp + fluid_mid), 0.0)
        total_one = ss[0] + shear_one
        total_two = ss[1] + shear_two
        locked = jnp.sqrt(total_one * total_one + total_two * total_two + 1.0)
        scaled = 0.5 * jnp.exp(state_now / direct)
        floor_term = 4.0 * jnp.exp(-2.0 * state_now / direct)
        strength_rate = effective * direct
        for sweep in range(NEWTON):
            residual = strength_rate * inverse_sinh(scaled * slip_rate) + damping * slip_rate - locked
            slope = strength_rate / jnp.sqrt(floor_term + slip_rate * slip_rate) + damping
            slip_rate = slip_rate - residual / slope
        steady = friction_ref - (evolution - direct) * 0.5 * jnp.log(
            slip_rate * slip_rate + rate_floor
        )
        state_now = steady + (state_now - steady) * jnp.exp(-jnp.abs(slip_rate) * widths[j] / slip)
        strength = locked - damping * slip_rate
        traction_one = strength * total_one / locked - ss[0]
        traction_two = strength * total_two / locked - ss[1]
        h = widths[j]
        for side, t, sign in ((0, m, 1.0), (1, n, -1.0)):
            d0 = normal_mid - t[0]
            d1 = traction_one - t[1]
            d2 = traction_two - t[2]
            d6 = fluid_mid - t[6]
            changes = [
                d0,
                d1,
                d2,
                d0 * (sign / impedance_normal),
                d1 * (sign / impedance_shear),
                d2 * (sign / impedance_shear),
                d6,
                d6 * (sign / impedance_fluid),
            ]
            for i in range(8):
                back[side][i] = back[side][i] + h * changes[i]
    return slip_rate, state_now, back[0], back[1]


def fault_body(
    minus_ref,
    plus_ref,
    arr_ref,
    jq_ref,
    sp_ref,
    rb_ref,
    ns_ref,
    ss_ref,
    pp_ref,
    rate_ref,
    state_ref,
    direct_ref,
    evol_ref,
    slip_ref,
    ret_ref,
    rate_out,
    state_out,
    table_ref,
    picked_ref,
    trace_ref,
    rows_ref,
):
    slots = table_ref.shape[0] // 8
    sides = picked_ref.shape[0] // 8
    faces = sides // 2
    for j in range(3):
        table_ref[pl.ds(j, slots, stride=8), :] = arr_ref[:, :, 128 * j : 128 * (j + 1)].reshape(
            slots, 128
        )

    slot_ids = [ref[s] for ref in (minus_ref, plus_ref) for s in range(faces)]
    copy_rows([slot * 8 for slot in slot_ids], table_ref, picked_ref)
    taylor, widths = time_tables()
    columns = []
    for c in range(sides // 128):
        columns.append(
            jnp.concatenate(
                [picked_ref[pl.ds(1024 * c + j, 128, stride=8), :].T for j in range(3)], axis=0
            )
        )
    stacked = jnp.concatenate(columns, axis=1)
    current = stacked[:ROWS]
    geo = [stacked[ROWS + k : ROWS + k + 1] for k in range(9)]
    for m in range(ORDER):
        if m > 0:
            current = derivative(current, geo, jq_ref[...], sp_ref[...], 3)
        trace_ref[m] = part_product(rb_ref[...], [[x] for x in parts(current, 3)], 3)

    def trace_of(side):
        def get(i, j):
            cols = slice(side * faces, (side + 1) * faces)
            value = trace_ref[0, 16 * i : 16 * i + 16, cols] * taylor[j][0]
            for m in range(1, ORDER):
                value = value + taylor[j][m] * trace_ref[m, 16 * i : 16 * i + 16, cols]
            return value

        return get

    slip_rate, state_now, back_minus, back_plus = friction(
        trace_of(0),
        trace_of(1),
        ns_ref[...],
        (ss_ref[0], ss_ref[1]),
        pp_ref[...],
        rate_ref[...],
        state_ref[...],
        direct_ref[...],
        evol_ref[...],
        slip_ref[...],
        widths,
    )
    rate_out[...] = slip_rate
    state_out[...] = state_now
    for side, back in ((0, back_minus), (1, back_plus)):
        stacked = jnp.concatenate(back, axis=0)
        for c in range(faces // 128):
            rows_ref[pl.ds(side * faces + 128 * c, 128), :] = stacked[:, 128 * c : 128 * (c + 1)].T
    ret_ref[...] = jnp.zeros_like(ret_ref)

    for s in range(sides):
        ret_ref[pl.ds(slot_ids[s], 1), :] = rows_ref[s : s + 1, :]


def fault(minus_slot, plus_slot, arrived, mats, fields):
    slots = arrived.shape[0] * arrived.shape[1]
    faces = minus_slot.shape[0]
    sides = 2 * faces
    point = jax.ShapeDtypeStruct((POINTS, faces), f32)
    vmem = pl.BlockSpec(memory_space=pltpu.VMEM)
    return pl.pallas_call(
        fault_body,
        out_shape=[jax.ShapeDtypeStruct((slots, 128), f32), point, point],
        in_specs=[pl.BlockSpec(memory_space=pltpu.SMEM)] * 2 + [vmem] * (1 + len(mats) + len(fields)),
        out_specs=[vmem] * 3,
        scratch_shapes=[
            pltpu.VMEM((slots * 8, 128), f32),
            pltpu.VMEM((sides * 8, 128), f32),
            pltpu.VMEM((ORDER, 128, sides), f32),
            pltpu.VMEM((sides, 128), f32),
        ],
        compiler_params=params(),
        name="fault",
    )(minus_slot, plus_slot, arrived, *mats, *fields)


def beside_body(
    index_ref,
    integ_ref,
    low_ref,
    high_ref,
    part_ref,
    scale_ref,
    fa_ref,
    fb_ref,
    jp_ref,
    out_ref,
    table_ref,
    picked_ref,
):
    step = pl.program_id(0)
    elems = integ_ref.shape[1]

    @pl.when(step == 0)
    def _():
        for source, first, count in (
            (low_ref, 0, GHOST),
            (integ_ref, GHOST, elems),
            (high_ref, GHOST + elems, GHOST),
        ):
            for c in range(count // 128):
                field = source[:, 128 * c : 128 * (c + 1)]
                for j, tiles in enumerate(GROUPS):
                    rows = pick(field, tiles)
                    pad = 128 - 8 * len(tiles)
                    stacked = jnp.concatenate(rows + [jnp.zeros((pad, 128), f32)], axis=0)
                    table_ref[pl.ds(8 * (first + 128 * c) + j, 128, stride=8), :] = stacked.T
        table_ref[pl.ds(8 * (elems + 2 * GHOST), 8), :] = jnp.zeros((8, 128), f32)

    scale = [scale_ref[f : f + 1, :] for f in range(4)]
    total = [None] * (PAIRS * QUADS)
    for f in range(FACES):
        copy_rows([index_ref[f, s] for s in range(COLS)], table_ref, picked_ref)
        for j, tiles in enumerate(GROUPS):
            hi, lo = parts(picked_ref[pl.ds(j, COLS, stride=8), :], 2)
            right = jnp.concatenate([hi, lo], axis=1).astype(bf16)
            out = dot_t(fb_ref[f] if j == 2 else fa_ref[f], right)
            half = out.shape[0] // 2
            out = scale[f] * (out[:half] + out[half:])
            for k, t in enumerate(tiles):
                value = out[8 * k : 8 * k + 8]
                total[t] = value if total[t] is None else total[t] + value
    hi, lo = parts(jnp.concatenate(total, axis=0), 2)
    for k in range(QUADS):
        out = part_product(jp_ref[...], [[quad(hi, k)], [quad(lo, k)]], 2)
        rows = slice(QUAD_ROWS * k, QUAD_ROWS * (k + 1))
        out_ref[rows, :] = part_ref[rows, :] + out


def beside(neighbours, integrated, low, high, partial, face_scale, mats):
    elems = integrated.shape[1]
    block = pl.BlockSpec((ROWS, COLS), lambda i: (0, i))
    return pl.pallas_call(
        beside_body,
        grid=(elems // COLS,),
        out_shape=jax.ShapeDtypeStruct((ROWS, elems), f32),
        in_specs=[
            pl.BlockSpec((FACES, COLS), lambda i: (0, i), memory_space=pltpu.SMEM),
            whole(integrated),
            whole(low),
            whole(high),
            block,
            pl.BlockSpec((FACES, COLS), lambda i: (0, i)),
        ]
        + [whole(m) for m in mats],
        out_specs=block,
        scratch_shapes=[
            pltpu.VMEM(((elems + 2 * GHOST + 8) * 8, 128), f32),
            pltpu.VMEM((COLS * 8, 128), f32),
        ],
        compiler_params=params(),
        name="beside",
    )(neighbours, integrated, low, high, partial, face_scale, *mats)


def lift_body(elem_ref, back_ref, part_ref, scale_ref, lift_ref, out_ref, values_ref):
    step = pl.program_id(0)
    cols = out_ref.shape[2]
    capacity, owners = elem_ref.shape
    chosen = []

    @pl.when(step == 0)
    def _():
        for c in range(capacity):
            hi, lo = parts(back_ref[pl.ds(c, owners, stride=capacity), :], 2)
            values_ref[owners * c : owners * (c + 1), :] = jnp.concatenate([hi, lo], axis=1).astype(
                bf16
            )

    ids = lax.broadcasted_iota(jnp.int32, (cols, owners), 0) + step * cols
    for c in range(capacity):
        chosen.append(ones_where(ids == elem_ref[c : c + 1, :]).astype(bf16))
    summed = dot(jnp.concatenate(chosen, axis=1), values_ref[...])
    hi, lo = parts(summed[:, :128] + summed[:, 128:], 2)
    out = dot_t(lift_ref[...], jnp.concatenate([hi, lo], axis=1).astype(bf16))
    out = part_ref[...] + scale_ref[FACES - 1 : FACES, :] * (out[:ROWS] + out[ROWS:])
    for q in range(13):
        for k in range(QUADS):
            at = QUAD_ROWS * k + 4 * q
            out_ref[q, 4 * k : 4 * k + 4, :] = out[at : at + 4]


def lift(elem_row, back, partial, face_scale, matrix):
    elems = partial.shape[1]
    cols = 1024
    return pl.pallas_call(
        lift_body,
        grid=(elems // cols,),
        out_shape=jax.ShapeDtypeStruct((QUANT, BASIS, elems), f32),
        in_specs=[
            whole(elem_row),
            whole(back),
            pl.BlockSpec((ROWS, cols), lambda i: (0, i)),
            pl.BlockSpec((FACES, cols), lambda i: (0, i)),
            whole(matrix),
        ],
        out_specs=pl.BlockSpec((QUANT, BASIS, cols), lambda i: (0, 0, i)),
        scratch_shapes=[pltpu.VMEM(back.shape[:1] + (256,), bf16)],
        compiler_params=params(),
        name="lift",
    )(elem_row, back, partial, face_scale, matrix)


def shards(
    coefficients,
    geometry,
    face_scale,
    neighbours,
    stiffness,
    face_minus,
    face_plus,
    jacobians,
    flux_minus,
    flux_plus,
    face_basis,
    rotation,
    lift_quantity,
    lift_basis,
    send_elements,
    send_count,
    minus_slot,
    plus_slot,
    normal_stress,
    shear_stress,
    pore_pressure,
    initial_rate,
    initial_state,
    direct_effect,
    evolution_effect,
    slip_length,
):
    part_count = send_elements.shape[1]
    capacity = send_elements.shape[2]
    slot_total = part_count * capacity
    slot_elements = jnp.transpose(send_elements[0])
    outgoing = send(slot_elements, coefficients, geometry)
    arrived = lax.all_to_all(outgoing, AXES, split_axis=0, concat_axis=0, tiled=True)
    mats = prep(
        stiffness,
        jnp.transpose(face_minus, (1, 0, 2)),
        jnp.transpose(face_plus, (1, 0, 2)),
        jacobians,
        flux_minus,
        flux_plus,
        face_basis,
        rotation,
        lift_quantity.T,
        lift_basis.T,
    )
    jq, sp, ex, ju, fa, fb, jp, jq3, sp3, rb, lift_matrix = mats
    integrated, partial, first, last, rows = main(
        coefficients, geometry, face_scale, neighbours, (jq, sp, ex, ju)
    )
    arrived, first, last = lax.optimization_barrier((arrived, first, last))
    count = part_count
    forward = [(i, i + 1) for i in range(count - 1)]
    backward = [(target, source) for source, target in forward]
    low = lax.ppermute(last, AXES, forward)
    high = lax.ppermute(first, AXES, backward)
    returned, slip_rate, fault_state = fault(
        minus_slot,
        plus_slot,
        arrived,
        (jq3, sp3, rb),
        (
            normal_stress,
            shear_stress,
            pore_pressure,
            initial_rate,
            initial_state,
            direct_effect,
            evolution_effect,
            slip_length,
        ),
    )
    returned, low, high = lax.optimization_barrier((returned, low, high))
    back = lax.all_to_all(
        returned.reshape(part_count, capacity, 128), AXES, split_axis=0, concat_axis=0, tiled=True
    )
    partial = beside(rows, integrated, low, high, partial, face_scale, (fa, fb, jp))
    updated = lift(
        slot_elements,
        back.reshape(slot_total, 128),
        partial,
        face_scale,
        lift_matrix,
    )
    return (updated, slip_rate, fault_state)


def solution(mesh):
    cols = P(None, AXES)
    in_specs = (
        P(None, None, AXES),
        P(None, None, AXES),
        cols,
        cols,
        *(P() for _ in range(10)),
        P(AXES, None, None),
        P(AXES, None),
        P(AXES),
        P(AXES),
        cols,
        P(None, None, AXES),
        *(cols for _ in range(6)),
    )
    out_specs = (P(None, None, AXES), cols, cols)
    return jax.shard_map(shards, mesh=mesh, in_specs=in_specs, out_specs=out_specs, check_vma=False)
```

```python
import math

import jax
import jax.numpy as jnp
import numpy as np
from jax import lax
from jax.experimental import pallas as pl
from jax.experimental.pallas import tpu as pltpu
from jax.sharding import PartitionSpec as P

QUANT = 13
BASIS = 20
ORDER = 4
FACES = 4
POINTS = 16
TPOINTS = 4
FQUANT = 8
NEWTON = 6
GHOST = 256
COLS = 1024
MAIN_COLS = 1024

time_step = 0.5
friction_ref = 0.6
impedance_normal = 2.0
impedance_shear = 1.2
impedance_fluid = 0.8
rate_floor = 0.01
gauss_inner = 0.3399810435848563
gauss_outer = 0.8611363115940526
weight_inner = 0.6521451548625461
weight_outer = 0.3478548451374538

f32 = jnp.float32
bf16 = jnp.bfloat16
AXES = ("space", "sub")
VMEM_LIMIT = 56 * 1024 * 1024

QUADS = 5
PAIRS = 7
ROWS = 280
QUAD_ROWS = 56
PAIR_ROWS = 40


def pair_tiles(p):
    return [PAIRS * k + p for k in range(QUADS)]


GROUPS = tuple([t for p in pairs for t in pair_tiles(p)] for pairs in ((0, 1), (2, 3), (4, 5, 6)))


def time_tables():
    gauss_nodes = [-gauss_outer, -gauss_inner, gauss_inner, gauss_outer]
    gauss_weights = [weight_outer, weight_inner, weight_inner, weight_outer]
    time_points = [time_step * (1.0 + node_value) / 2.0 for node_value in gauss_nodes]
    widths = [time_step * weight_value / 2.0 for weight_value in gauss_weights]
    taylor = [
        [float(np.float32(point_value**power / math.factorial(power))) for power in range(ORDER)]
        for point_value in time_points
    ]
    return taylor, [float(width_value) for width_value in widths]


def block_of(r, width):
    at = (r * (-(-(1 << 20) // width))) >> 20
    return at, r - at * width


def quad_rows(r):
    return r >> 2, r & 3


def pair_rows(r):
    return (r >> 2) & 1, 4 * (r >> 3) + (r & 3)


def group_rows(pairs):
    def get(r):
        p, local = block_of(r, PAIR_ROWS)
        q, b = pair_rows(local)
        beyond = r >= PAIR_ROWS * pairs
        return jnp.where(beyond, -1, 2 * p + q), jnp.where(beyond, -1, b)

    return get


def field_rows(r):
    k, local = block_of(r, QUAD_ROWS)
    return local >> 2, 4 * k + (local & 3)


def ones_where(cond):
    return jnp.where(cond, 1.0, 0.0)


def dot(a, b):
    return lax.dot_general(a, b, (((1,), (0,)), ((), ())), preferred_element_type=f32)


def dot_t(a, b):
    return lax.dot_general(a, b, (((1,), (1,)), ((), ())), preferred_element_type=f32)


def parts(x, count):
    out = []
    for _ in range(count):
        hi = x.astype(bf16)
        out.append(hi.astype(f32))
        x = x - out[-1]
    return out


def stack_parts(mats, count, pitch):
    pieces = []
    for mat in mats:
        pad = jnp.zeros((pitch - mat.shape[0], mat.shape[1]), f32)
        for part in parts(mat, count):
            pieces += [part, pad]
    return jnp.concatenate(pieces, axis=0).astype(bf16)


def block_matrix(
    data, pitch, count, layout, row_w, row_blocks, col_w, col_blocks, on_q, triple=False, col_pitch=0
):
    size = data.shape[1]
    mats = data.shape[0] // (pitch * count)
    row_parts = 1 if triple else count
    col_parts = 3 if triple else count
    rows = row_parts * row_blocks * row_w
    col_pitch = col_pitch or col_blocks * col_w
    cols = col_parts * col_pitch
    r = lax.broadcasted_iota(jnp.int32, (rows, 1), 0)
    c = lax.broadcasted_iota(jnp.int32, (1, cols), 1)
    row_at, row_local = block_of(r, row_w)
    col_part, within = block_of(c, col_pitch)
    col_block, col_local = block_of(within, col_w)
    row_q, row_b = layout(row_local)
    col_q, col_b = layout(col_local)
    row_i, row_m = (row_q, row_b) if on_q else (row_b, row_q)
    col_i, col_m = (col_q, col_b) if on_q else (col_b, col_q)
    row_part, row_block = block_of(row_at, row_blocks)
    k = lax.broadcasted_iota(jnp.int32, (size, 1), 0)
    right = ones_where(k == col_i).astype(bf16)
    s = lax.broadcasted_iota(jnp.int32, (1, data.shape[0]), 1)
    mask = row_m == col_m
    if triple:
        s_block, s_local = block_of(s, pitch)
        s_mat = s_block >> 1
        left = ones_where((s_local == row_i) & (s_mat == row_block)).astype(bf16)
        t = lax.broadcasted_iota(jnp.int32, (data.shape[0], 1), 0)
        t_part = block_of(t, pitch)[0] & 1
        wide = dot(data, right)
        wide = jnp.where(t_part == (col_part & 1), wide, 0.0).astype(bf16)
        out = dot(left, wide)
    elif col_blocks == 1:
        left = ones_where(s == (row_block * count + row_part) * pitch + row_i).astype(bf16)
        out = dot(dot(left, data).astype(bf16), right)
        mask = mask & (row_part + col_part < count)
    else:
        s_local = block_of(s, pitch * count)[1]
        left = ones_where(s_local == row_part * pitch + row_i).astype(bf16)
        t = lax.broadcasted_iota(jnp.int32, (data.shape[0], 1), 0)
        wide = dot(data, right)
        wide = jnp.where(block_of(t, pitch * count)[0] == col_block, wide, 0.0).astype(bf16)
        out = dot(left, wide)
        mask = mask & (row_part + col_part < count)
    return jnp.where(mask, out, 0.0).astype(bf16)


def prep_body(
    stiff_ref,
    fm_ref,
    fp_ref,
    jac_ref,
    fluxm_ref,
    fluxp_ref,
    basis_ref,
    rot_ref,
    lq_ref,
    lb_ref,
    jq_ref,
    sp_ref,
    ex_ref,
    ju_ref,
    fa_ref,
    fb_ref,
    jp_ref,
    jq3_ref,
    sp3_ref,
    rb_ref,
    lift_ref,
):
    jac = [jac_ref[x] for x in range(3)]
    minus_stiff = [-stiff_ref[d] for d in range(3)]
    jac_data = stack_parts(jac, 2, 16)
    jq_ref[...] = block_matrix(jac_data, 16, 2, quad_rows, 56, 3, 56, 1, True, True)
    jac_data = stack_parts(jac, 3, 16)
    jq3_ref[...] = block_matrix(jac_data, 16, 3, quad_rows, 56, 3, 56, 1, True)
    for count, ref in ((2, sp_ref), (3, sp3_ref)):
        stiff_data = stack_parts(minus_stiff, count, 24)
        ref[...] = block_matrix(
            stiff_data, 24, count, pair_rows, 40, 1, 40, 3, False, col_pitch=128
        )
    last_data = stack_parts(jac + [-fluxm_ref[...]], 2, 16)
    ju_ref[...] = block_matrix(last_data, 16, 2, quad_rows, 56, 1, 56, 4, True)
    plus_data = stack_parts([-fluxp_ref[...]], 2, 16)
    jp_ref[...] = block_matrix(plus_data, 16, 2, quad_rows, 56, 1, 56, 1, True)
    for f in range(4):
        face_data = stack_parts([fp_ref[:, f, :]], 2, 24)
        fa_ref[f] = block_matrix(face_data, 24, 2, group_rows(2), 80, 1, 128, 1, False)
        fb_ref[f] = block_matrix(face_data, 24, 2, group_rows(3), 120, 1, 128, 1, False)
    expand = [stiff_ref[d].T for d in range(3)] + [fm_ref[:, f, :] for f in range(4)]
    expand_data = stack_parts(expand, 2, 24)
    ex_ref[...] = block_matrix(expand_data, 24, 2, pair_rows, 40, 7, 40, 1, False, True)

    def spread(x, right):
        return sum(dot(part.astype(bf16), right) for part in reversed(parts(x, 3)))

    column = lax.broadcasted_iota(jnp.int32, (1, 3 * ROWS), 1)
    column_part, column = block_of(column, ROWS)
    column_q, column_b = field_rows(column)
    q_id = lax.broadcasted_iota(jnp.int32, (QUANT, 1), 0)
    b_id = lax.broadcasted_iota(jnp.int32, (BASIS, 1), 0)
    rot = spread(rot_ref[...], ones_where(q_id == column_q).astype(bf16))
    bas = spread(basis_ref[...], ones_where(b_id == column_b).astype(bf16))
    full = jnp.concatenate([rot[i : i + 1, :] * bas for i in range(8)], axis=0)
    rows = [jnp.where(column_part < 3 - h, part, 0.0) for h, part in enumerate(parts(full, 3))]
    rb_ref[...] = jnp.concatenate(rows, axis=0).astype(bf16)
    lane = lax.broadcasted_iota(jnp.int32, (1, 256), 1)
    i_id = lax.broadcasted_iota(jnp.int32, (FQUANT, 1), 0)
    k_id = lax.broadcasted_iota(jnp.int32, (POINTS, 1), 0)
    lq = spread(lq_ref[...].T, ones_where(i_id == ((lane >> 4) & 7)).astype(bf16))
    lb = spread(lb_ref[...].T, ones_where(k_id == (lane & 15)).astype(bf16))
    pieces = []
    upper = lax.broadcasted_iota(jnp.int32, (8, 256), 0) < 4
    for k in range(QUADS):
        quad = lb[4 * k : 4 * k + 4, :]
        quad = jnp.concatenate([quad, quad], axis=0)
        for p in range(PAIRS):
            first = lq[2 * p : 2 * p + 1, :]
            second = lq[2 * p + 1 : 2 * p + 2, :] if p < 6 else jnp.zeros_like(first)
            pieces.append(jnp.where(upper, first, second) * quad)
    hi, lo = parts(jnp.concatenate(pieces, axis=0), 2)
    lo = jnp.where(lane < 128, lo, 0.0)
    lift_ref[...] = jnp.concatenate([hi, lo], axis=0).astype(bf16)


PREP_SHAPES = (
    (168, 168),
    (80, 256),
    (280, 120),
    (112, 448),
    (4, 160, 256),
    (4, 240, 256),
    (112, 112),
    (504, 168),
    (120, 384),
    (384, 3 * ROWS),
    (2 * ROWS, 256),
)


def params(**kw):
    return pltpu.CompilerParams(vmem_limit_bytes=VMEM_LIMIT, **kw)


def prep(*matrices):
    return pl.pallas_call(
        prep_body,
        out_shape=[jax.ShapeDtypeStruct(s, bf16) for s in PREP_SHAPES],
        compiler_params=params(),
        name="prep",
    )(*matrices)


def pick(x, tiles):
    return [x[8 * t : 8 * t + 8, :] for t in tiles]


def stacked_parts(blocks, count):
    x = jnp.concatenate(blocks, axis=0)
    out = []
    for h in range(count):
        out.append(x.astype(bf16))
        if h < count - 1:
            x = x - out[-1].astype(f32)
    return jnp.concatenate(out, axis=0)


def fold(out, count):
    size = out.shape[0] // count
    total = out[(count - 1) * size :]
    for h in reversed(range(count - 1)):
        total = out[h * size : (h + 1) * size] + total
    return total


def part_product(matrix, blocks, count):
    right = jnp.concatenate([b for part in blocks for b in part], axis=0)
    return fold(dot(matrix, right.astype(bf16)), count)


def quad(x, k):
    return x[QUAD_ROWS * k : QUAD_ROWS * (k + 1)]


def derivative(field, geo, jq, sp, count):
    pieces = parts(field, count)
    blocks = [[], [], []]
    for k in range(QUADS):
        if count == 2:
            hi, lo = quad(pieces[0], k), quad(pieces[1], k)
            out = dot(jq, jnp.concatenate([hi, hi, lo], axis=0).astype(bf16))
        else:
            out = part_product(jq, [[quad(x, k)] for x in pieces], count)
        for d in range(3):
            blocks[d].append(
                geo[3 * d] * quad(out, 0) + geo[3 * d + 1] * quad(out, 1) + geo[3 * d + 2] * quad(out, 2)
            )
    directed = [jnp.concatenate(block, axis=0) for block in blocks]
    pad = [jnp.zeros((8, field.shape[1]), f32)]
    tiles = [None] * (PAIRS * QUADS)
    for p in range(PAIRS):
        chosen = pair_tiles(p)
        right = stacked_parts([t for d in range(3) for t in pick(directed[d], chosen)] + pad, count)
        out = fold(dot(sp, right), count)
        for k, t in enumerate(chosen):
            tiles[t] = out[8 * k : 8 * k + 8, :]
    return jnp.concatenate(tiles, axis=0)


def load_field(ref):
    tiles = []
    for k in range(QUADS):
        for p in range(PAIRS):
            low = ref[2 * p, 4 * k : 4 * k + 4, :]
            high = ref[2 * p + 1, 4 * k : 4 * k + 4, :] if p < 6 else jnp.zeros_like(low)
            tiles.append(jnp.concatenate([low, high], axis=0))
    return jnp.concatenate(tiles, axis=0)


def copy_rows(sources, table_ref, picked_ref):
    for base in range(0, len(sources), 32):
        got = [
            table_ref[pl.ds(pl.multiple_of(row, 8), 8), :] for row in sources[base : base + 32]
        ]
        for k, value in enumerate(got):
            picked_ref[8 * (base + k) : 8 * (base + k) + 8, :] = value


def send_body(index_ref, coef_ref, geo_ref, out_ref, table_ref, picked_ref):
    elems = coef_ref.shape[2]
    slots = picked_ref.shape[0] // 8
    for c in range(elems // 128):
        cols = pl.ds(128 * c, 128)
        field = load_field(coef_ref.at[:, :, cols])
        geo = [geo_ref[d, x : x + 1, cols] for d in range(3) for x in range(3)]
        geo = jnp.concatenate(geo + [jnp.zeros((384 - ROWS - 9, 128), f32)], axis=0)
        stacked = jnp.concatenate([field, geo], axis=0)
        for j in range(3):
            table_ref[pl.ds(128 * 8 * c + j, 128, stride=8), :] = stacked[128 * j : 128 * (j + 1)].T

    copy_rows(
        [index_ref[s % 8, s // 8] * 8 for s in range(slots)], table_ref, picked_ref
    )
    for j in range(3):
        out_ref[:, :, 128 * j : 128 * (j + 1)] = picked_ref[pl.ds(j, slots, stride=8), :].reshape(
            slots // 8, 8, 128
        )


def send(index, coefficients, geometry):
    elems = coefficients.shape[2]
    slots = index.shape[0] * index.shape[1]
    return pl.pallas_call(
        send_body,
        out_shape=jax.ShapeDtypeStruct((slots // 8, 8, 384), f32),
        in_specs=[
            pl.BlockSpec(memory_space=pltpu.SMEM),
            pl.BlockSpec(memory_space=pltpu.VMEM),
            pl.BlockSpec(memory_space=pltpu.VMEM),
        ],
        out_specs=pl.BlockSpec(memory_space=pltpu.VMEM),
        scratch_shapes=[pltpu.VMEM((elems * 8, 128), f32), pltpu.VMEM((slots * 8, 128), f32)],
        compiler_params=params(),
        name="send",
    )(index, coefficients, geometry)


STEP_WEIGHTS = [time_step ** (power + 1) / math.factorial(power + 1) for power in range(ORDER)]


def main_body(
    coef_ref,
    geo_ref,
    scale_ref,
    beside_ref,
    jq_ref,
    sp_ref,
    ex_ref,
    ju_ref,
    integ_ref,
    part_ref,
    first_ref,
    last_ref,
    row_ref,
):
    step = pl.program_id(0)
    row_ref[...] = beside_ref[...] * 8
    field = load_field(coef_ref)
    geo = [geo_ref[d, x : x + 1, :] for d in range(3) for x in range(3)]
    integ_ref[...] = STEP_WEIGHTS[0] * field
    current = field
    for power in range(1, ORDER):
        current = derivative(current, geo, jq_ref[...], sp_ref[...], 2)
        integ_ref[...] += STEP_WEIGHTS[power] * current
    integrated = integ_ref[...]

    @pl.when(step == 0)
    def _():
        first_ref[...] = integrated[:, :GHOST]

    @pl.when(step == pl.num_programs(0) - 1)
    def _():
        last_ref[...] = integrated[:, integrated.shape[1] - GHOST :]

    hi, lo = parts(integrated, 2)
    pieces = [[None] * (PAIRS * QUADS) for _ in range(4)]
    scale = [scale_ref[f : f + 1, :] for f in range(4)]
    for p in range(PAIRS):
        chosen = pair_tiles(p)
        right = pick(hi, chosen) + pick(hi, chosen) + pick(lo, chosen)
        out = dot(ex_ref[...], jnp.concatenate(right, axis=0).astype(bf16))
        blocks = [out[PAIR_ROWS * k : PAIR_ROWS * (k + 1)] for k in range(7)]
        results = [
            geo[x] * blocks[0] + geo[3 + x] * blocks[1] + geo[6 + x] * blocks[2] for x in range(3)
        ]
        results.append(
            scale[0] * blocks[3] + scale[1] * blocks[4] + scale[2] * blocks[5] + scale[3] * blocks[6]
        )
        for m in range(4):
            for k, t in enumerate(chosen):
                pieces[m][t] = results[m][8 * k : 8 * k + 8]
    joined = [jnp.concatenate(tiles, axis=0) for tiles in pieces]
    for k in range(QUADS):
        out = fold(dot(ju_ref[...], stacked_parts([quad(x, k) for x in joined], 2)), 2)
        rows = slice(QUAD_ROWS * k, QUAD_ROWS * (k + 1))
        part_ref[rows, :] = field[rows] + out


def whole(array):
    shape = array.shape
    return pl.BlockSpec(shape, lambda *_: (0,) * len(shape))


def main(coefficients, geometry, face_scale, neighbours, mats):
    elems = coefficients.shape[2]
    block = pl.BlockSpec((ROWS, MAIN_COLS), lambda i: (0, i))
    fixed = pl.BlockSpec((ROWS, GHOST), lambda i: (0, 0))
    field = jax.ShapeDtypeStruct((ROWS, elems), f32)
    rim = jax.ShapeDtypeStruct((ROWS, GHOST), f32)
    return pl.pallas_call(
        main_body,
        grid=(elems // MAIN_COLS,),
        out_shape=[field, field, rim, rim, jax.ShapeDtypeStruct(neighbours.shape, jnp.int32)],
        in_specs=[
            pl.BlockSpec((QUANT, BASIS, MAIN_COLS), lambda i: (0, 0, i)),
            pl.BlockSpec((3, 3, MAIN_COLS), lambda i: (0, 0, i)),
            pl.BlockSpec((FACES, MAIN_COLS), lambda i: (0, i)),
            pl.BlockSpec((FACES, MAIN_COLS), lambda i: (0, i)),
        ]
        + [whole(m) for m in mats],
        out_specs=[
            block,
            block,
            fixed,
            fixed,
            pl.BlockSpec((FACES, MAIN_COLS), lambda i: (0, i)),
        ],
        compiler_params=params(),
        name="main",
    )(coefficients, geometry, face_scale, neighbours, *mats)


def inverse_sinh(value):
    magnitude = jnp.abs(value)
    result = jnp.log(magnitude + jnp.sqrt(magnitude * magnitude + 1.0))
    return jnp.where(value < 0.0, -result, result)


def friction(minus, plus, ns, ss, pp, rate, state, direct, evolution, slip, widths):
    damping = 0.5 * impedance_shear
    slip_rate = rate
    state_now = state
    back = [[0.0] * 8, [0.0] * 8]
    for j in range(TPOINTS):
        m = [minus(i, j) for i in range(8)]
        n = [plus(i, j) for i in range(8)]
        normal_mid = 0.5 * (m[0] + n[0]) + 0.5 * impedance_normal * (n[3] - m[3])
        shear_one = 0.5 * (m[1] + n[1]) + 0.5 * impedance_shear * (n[4] - m[4])
        shear_two = 0.5 * (m[2] + n[2]) + 0.5 * impedance_shear * (n[5] - m[5])
        fluid_mid = 0.5 * (m[6] + n[6]) + 0.5 * impedance_fluid * (n[7] - m[7])
        effective = jnp.maximum(-(ns + normal_mid + pp + fluid_mid), 0.0)
        total_one = ss[0] + shear_one
        total_two = ss[1] + shear_two
        locked = jnp.sqrt(total_one * total_one + total_two * total_two + 1.0)
        scaled = 0.5 * jnp.exp(state_now / direct)
        floor_term = 4.0 * jnp.exp(-2.0 * state_now / direct)
        strength_rate = effective * direct
        for sweep in range(NEWTON):
            residual = strength_rate * inverse_sinh(scaled * slip_rate) + damping * slip_rate - locked
            slope = strength_rate / jnp.sqrt(floor_term + slip_rate * slip_rate) + damping
            slip_rate = slip_rate - residual / slope
        steady = friction_ref - (evolution - direct) * 0.5 * jnp.log(
            slip_rate * slip_rate + rate_floor
        )
        state_now = steady + (state_now - steady) * jnp.exp(-jnp.abs(slip_rate) * widths[j] / slip)
        strength = locked - damping * slip_rate
        traction_one = strength * total_one / locked - ss[0]
        traction_two = strength * total_two / locked - ss[1]
        h = widths[j]
        for side, t, sign in ((0, m, 1.0), (1, n, -1.0)):
            d0 = normal_mid - t[0]
            d1 = traction_one - t[1]
            d2 = traction_two - t[2]
            d6 = fluid_mid - t[6]
            changes = [
                d0,
                d1,
                d2,
                d0 * (sign / impedance_normal),
                d1 * (sign / impedance_shear),
                d2 * (sign / impedance_shear),
                d6,
                d6 * (sign / impedance_fluid),
            ]
            for i in range(8):
                back[side][i] = back[side][i] + h * changes[i]
    return slip_rate, state_now, back[0], back[1]


def fault_body(
    minus_ref,
    plus_ref,
    arr_ref,
    jq_ref,
    sp_ref,
    rb_ref,
    ns_ref,
    ss_ref,
    pp_ref,
    rate_ref,
    state_ref,
    direct_ref,
    evol_ref,
    slip_ref,
    ret_ref,
    rate_out,
    state_out,
    table_ref,
    picked_ref,
    trace_ref,
    rows_ref,
):
    slots = table_ref.shape[0] // 8
    sides = picked_ref.shape[0] // 8
    faces = sides // 2
    for j in range(3):
        table_ref[pl.ds(j, slots, stride=8), :] = arr_ref[:, :, 128 * j : 128 * (j + 1)].reshape(
            slots, 128
        )

    slot_ids = [ref[s] for ref in (minus_ref, plus_ref) for s in range(faces)]
    copy_rows([slot * 8 for slot in slot_ids], table_ref, picked_ref)
    taylor, widths = time_tables()
    columns = []
    for c in range(sides // 128):
        columns.append(
            jnp.concatenate(
                [picked_ref[pl.ds(1024 * c + j, 128, stride=8), :].T for j in range(3)], axis=0
            )
        )
    stacked = jnp.concatenate(columns, axis=1)
    current = stacked[:ROWS]
    geo = [stacked[ROWS + k : ROWS + k + 1] for k in range(9)]
    for m in range(ORDER):
        if m > 0:
            current = derivative(current, geo, jq_ref[...], sp_ref[...], 3)
        trace_ref[m] = part_product(rb_ref[...], [[x] for x in parts(current, 3)], 3)

    def trace_of(side):
        def get(i, j):
            cols = slice(side * faces, (side + 1) * faces)
            value = trace_ref[0, 16 * i : 16 * i + 16, cols] * taylor[j][0]
            for m in range(1, ORDER):
                value = value + taylor[j][m] * trace_ref[m, 16 * i : 16 * i + 16, cols]
            return value

        return get

    slip_rate, state_now, back_minus, back_plus = friction(
        trace_of(0),
        trace_of(1),
        ns_ref[...],
        (ss_ref[0], ss_ref[1]),
        pp_ref[...],
        rate_ref[...],
        state_ref[...],
        direct_ref[...],
        evol_ref[...],
        slip_ref[...],
        widths,
    )
    rate_out[...] = slip_rate
    state_out[...] = state_now
    for side, back in ((0, back_minus), (1, back_plus)):
        stacked = jnp.concatenate(back, axis=0)
        for c in range(faces // 128):
            rows_ref[pl.ds(side * faces + 128 * c, 128), :] = stacked[:, 128 * c : 128 * (c + 1)].T
    ret_ref[...] = jnp.zeros_like(ret_ref)

    for s in range(sides):
        ret_ref[pl.ds(slot_ids[s], 1), :] = rows_ref[s : s + 1, :]


def fault(minus_slot, plus_slot, arrived, mats, fields):
    slots = arrived.shape[0] * arrived.shape[1]
    faces = minus_slot.shape[0]
    sides = 2 * faces
    point = jax.ShapeDtypeStruct((POINTS, faces), f32)
    vmem = pl.BlockSpec(memory_space=pltpu.VMEM)
    return pl.pallas_call(
        fault_body,
        out_shape=[jax.ShapeDtypeStruct((slots, 128), f32), point, point],
        in_specs=[pl.BlockSpec(memory_space=pltpu.SMEM)] * 2 + [vmem] * (1 + len(mats) + len(fields)),
        out_specs=[vmem] * 3,
        scratch_shapes=[
            pltpu.VMEM((slots * 8, 128), f32),
            pltpu.VMEM((sides * 8, 128), f32),
            pltpu.VMEM((ORDER, 128, sides), f32),
            pltpu.VMEM((sides, 128), f32),
        ],
        compiler_params=params(),
        name="fault",
    )(minus_slot, plus_slot, arrived, *mats, *fields)


def beside_body(
    index_ref,
    integ_ref,
    low_ref,
    high_ref,
    part_ref,
    scale_ref,
    fa_ref,
    fb_ref,
    jp_ref,
    out_ref,
    table_ref,
    picked_ref,
):
    step = pl.program_id(0)
    elems = integ_ref.shape[1]

    @pl.when(step == 0)
    def _():
        for source, first, count in (
            (low_ref, 0, GHOST),
            (integ_ref, GHOST, elems),
            (high_ref, GHOST + elems, GHOST),
        ):
            for c in range(count // 128):
                field = source[:, 128 * c : 128 * (c + 1)]
                for j, tiles in enumerate(GROUPS):
                    rows = pick(field, tiles)
                    pad = 128 - 8 * len(tiles)
                    stacked = jnp.concatenate(rows + [jnp.zeros((pad, 128), f32)], axis=0)
                    table_ref[pl.ds(8 * (first + 128 * c) + j, 128, stride=8), :] = stacked.T
        table_ref[pl.ds(8 * (elems + 2 * GHOST), 8), :] = jnp.zeros((8, 128), f32)

    scale = [scale_ref[f : f + 1, :] for f in range(4)]
    total = [None] * (PAIRS * QUADS)
    for f in range(FACES):
        copy_rows([index_ref[f, s] for s in range(COLS)], table_ref, picked_ref)
        for j, tiles in enumerate(GROUPS):
            hi, lo = parts(picked_ref[pl.ds(j, COLS, stride=8), :], 2)
            right = jnp.concatenate([hi, lo], axis=1).astype(bf16)
            out = dot_t(fb_ref[f] if j == 2 else fa_ref[f], right)
            half = out.shape[0] // 2
            out = scale[f] * (out[:half] + out[half:])
            for k, t in enumerate(tiles):
                value = out[8 * k : 8 * k + 8]
                total[t] = value if total[t] is None else total[t] + value
    hi, lo = parts(jnp.concatenate(total, axis=0), 2)
    for k in range(QUADS):
        out = part_product(jp_ref[...], [[quad(hi, k)], [quad(lo, k)]], 2)
        rows = slice(QUAD_ROWS * k, QUAD_ROWS * (k + 1))
        out_ref[rows, :] = part_ref[rows, :] + out


def beside(neighbours, integrated, low, high, partial, face_scale, mats):
    elems = integrated.shape[1]
    block = pl.BlockSpec((ROWS, COLS), lambda i: (0, i))
    return pl.pallas_call(
        beside_body,
        grid=(elems // COLS,),
        out_shape=jax.ShapeDtypeStruct((ROWS, elems), f32),
        in_specs=[
            pl.BlockSpec((FACES, COLS), lambda i: (0, i), memory_space=pltpu.SMEM),
            whole(integrated),
            whole(low),
            whole(high),
            block,
            pl.BlockSpec((FACES, COLS), lambda i: (0, i)),
        ]
        + [whole(m) for m in mats],
        out_specs=block,
        scratch_shapes=[
            pltpu.VMEM(((elems + 2 * GHOST + 8) * 8, 128), f32),
            pltpu.VMEM((COLS * 8, 128), f32),
        ],
        compiler_params=params(),
        name="beside",
    )(neighbours, integrated, low, high, partial, face_scale, *mats)


def lift_body(elem_ref, back_ref, part_ref, scale_ref, lift_ref, out_ref, values_ref):
    step = pl.program_id(0)
    cols = out_ref.shape[2]
    capacity, owners = elem_ref.shape
    chosen = []

    @pl.when(step == 0)
    def _():
        for c in range(capacity):
            hi, lo = parts(back_ref[pl.ds(c, owners, stride=capacity), :], 2)
            values_ref[owners * c : owners * (c + 1), :] = jnp.concatenate([hi, lo], axis=1).astype(
                bf16
            )

    ids = lax.broadcasted_iota(jnp.int32, (cols, owners), 0) + step * cols
    for c in range(capacity):
        chosen.append(ones_where(ids == elem_ref[c : c + 1, :]).astype(bf16))
    summed = dot(jnp.concatenate(chosen, axis=1), values_ref[...])
    hi, lo = parts(summed[:, :128] + summed[:, 128:], 2)
    out = dot_t(lift_ref[...], jnp.concatenate([hi, lo], axis=1).astype(bf16))
    out = part_ref[...] + scale_ref[FACES - 1 : FACES, :] * (out[:ROWS] + out[ROWS:])
    for q in range(13):
        for k in range(QUADS):
            at = QUAD_ROWS * k + 4 * q
            out_ref[q, 4 * k : 4 * k + 4, :] = out[at : at + 4]


def lift(elem_row, back, partial, face_scale, matrix):
    elems = partial.shape[1]
    cols = 1024
    return pl.pallas_call(
        lift_body,
        grid=(elems // cols,),
        out_shape=jax.ShapeDtypeStruct((QUANT, BASIS, elems), f32),
        in_specs=[
            whole(elem_row),
            whole(back),
            pl.BlockSpec((ROWS, cols), lambda i: (0, i)),
            pl.BlockSpec((FACES, cols), lambda i: (0, i)),
            whole(matrix),
        ],
        out_specs=pl.BlockSpec((QUANT, BASIS, cols), lambda i: (0, 0, i)),
        scratch_shapes=[pltpu.VMEM(back.shape[:1] + (256,), bf16)],
        compiler_params=params(),
        name="lift",
    )(elem_row, back, partial, face_scale, matrix)


def shards(
    coefficients,
    geometry,
    face_scale,
    neighbours,
    stiffness,
    face_minus,
    face_plus,
    jacobians,
    flux_minus,
    flux_plus,
    face_basis,
    rotation,
    lift_quantity,
    lift_basis,
    send_elements,
    send_count,
    minus_slot,
    plus_slot,
    normal_stress,
    shear_stress,
    pore_pressure,
    initial_rate,
    initial_state,
    direct_effect,
    evolution_effect,
    slip_length,
):
    part_count = send_elements.shape[1]
    capacity = send_elements.shape[2]
    slot_total = part_count * capacity
    slot_elements = jnp.transpose(send_elements[0])
    outgoing = send(slot_elements, coefficients, geometry)
    arrived = lax.all_to_all(outgoing, AXES, split_axis=0, concat_axis=0, tiled=True)
    mats = prep(
        stiffness,
        jnp.transpose(face_minus, (1, 0, 2)),
        jnp.transpose(face_plus, (1, 0, 2)),
        jacobians,
        flux_minus,
        flux_plus,
        face_basis,
        rotation,
        lift_quantity.T,
        lift_basis.T,
    )
    jq, sp, ex, ju, fa, fb, jp, jq3, sp3, rb, lift_matrix = mats
    integrated, partial, first, last, rows = main(
        coefficients, geometry, face_scale, neighbours, (jq, sp, ex, ju)
    )
    arrived, first, last = lax.optimization_barrier((arrived, first, last))
    count = part_count
    forward = [(i, i + 1) for i in range(count - 1)]
    backward = [(target, source) for source, target in forward]
    low = lax.ppermute(last, AXES, forward)
    high = lax.ppermute(first, AXES, backward)
    returned, slip_rate, fault_state = fault(
        minus_slot,
        plus_slot,
        arrived,
        (jq3, sp3, rb),
        (
            normal_stress,
            shear_stress,
            pore_pressure,
            initial_rate,
            initial_state,
            direct_effect,
            evolution_effect,
            slip_length,
        ),
    )
    returned, low, high = lax.optimization_barrier((returned, low, high))
    back = lax.all_to_all(
        returned.reshape(part_count, capacity, 128), AXES, split_axis=0, concat_axis=0, tiled=True
    )
    partial = beside(rows, integrated, low, high, partial, face_scale, (fa, fb, jp))
    updated = lift(
        slot_elements,
        back.reshape(slot_total, 128),
        partial,
        face_scale,
        lift_matrix,
    )
    return (updated, slip_rate, fault_state)


def solution(mesh):
    cols = P(None, AXES)
    in_specs = (
        P(None, None, AXES),
        P(None, None, AXES),
        cols,
        cols,
        *(P() for _ in range(10)),
        P(AXES, None, None),
        P(AXES, None),
        P(AXES),
        P(AXES),
        cols,
        P(None, None, AXES),
        *(cols for _ in range(6)),
    )
    out_specs = (P(None, None, AXES), cols, cols)
    return jax.shard_map(shards, mesh=mesh, in_specs=in_specs, out_specs=out_specs, check_vma=False)
```
